512 devices in a mesh: seq: 512 (over x, z, y, core).
Axes of the slice: x: 4, y: 8, z: 8, core: 2. Of those that a mesh axis runs over, the one named last changes fastest.
Arguments:
- query: bfloat16 [65536, 384], P('seq'), may hold values from -6 to 6
- keys: bfloat16 [65536, 384], P('seq'), may hold values from -6 to 6
- values: bfloat16 [65536, 384], P('seq'), may hold values from -6 to 6
- grad_out: bfloat16 [65536, 384], P('seq'), may hold values from -6 to 6
Outputs:
- attended: bfloat16 [65536, 384], P('seq')
- grad_query: bfloat16 [65536, 384], P('seq')
- grad_keys: bfloat16 [65536, 384], P('seq')
- grad_values: bfloat16 [65536, 384], P('seq')
The draws below stay inside these ranges and needn't reach their ends.
All inputs are finite; a program needn't handle non-finite values.
Results may differ from the reference program's by a relative error of at most 0.024.
Values may be sent and summed in bfloat16 or wider, within the bound.
No kernel may reach another device: no remote copies, remote signals or barrier semaphores. Data moves between devices by JAX's collectives and lax.ppermute only.
A program may use at most 64 MiB of HBM per device.

```python
from functools import reduce
import jax
import jax.numpy as jnp
from jax import lax

HEADS = 6
HD = 64
SEG = 512
D = 384
TOKENS = 65536
LEVELS = 5


def draw_query(key, part):
    key = jax.random.fold_in(key, 7)
    drawn = jnp.clip(jax.random.normal(key, (TOKENS, D), jnp.float32), -6.0, 6.0)
    return drawn.astype(jnp.bfloat16)


def draw_keys(key, part):
    key = jax.random.fold_in(key, 13)
    drawn = jnp.clip(jax.random.normal(key, (TOKENS, D), jnp.float32), -6.0, 6.0)
    return drawn.astype(jnp.bfloat16)


def steps_of(own_key, dims, pieces, low, largest):
    level, own = 1.0, jax.random.fold_in(own_key, 6)
    for dim, parts in pieces:
        draws = jnp.exp(jax.random.uniform(jax.random.fold_in(own, dim), (parts,), jnp.float32, low / len(pieces), largest / len(pieces)))
        level = level * jnp.repeat(draws, dims[dim] // parts).reshape([-1 if axis == dim else 1 for axis in range(len(dims))])
    return level


def scatter_about(own_key, extent, scale, most, pieces=(), dtype=jnp.bfloat16):
    array = scale * jax.random.normal(own_key, extent, jnp.float32)
    if pieces:
        array = array * steps_of(own_key, extent, pieces, -0.22, 0.18)
    return jnp.clip(array, -most, most).astype(dtype)


def setup_inputs(seed: int = 0) -> dict:
    seeds = jax.random.split(jax.random.key(seed), 5)
    query = draw_query(jax.random.fold_in(seeds[4], 71), 0)
    keys = draw_keys(jax.random.fold_in(seeds[4], 71), 0)
    values = scatter_about(seeds[2], (TOKENS, D), 1.0, 6.0, ((0, 512),))
    grad_out = scatter_about(seeds[3], (TOKENS, D), 1.0, 6.0, ((0, 512),))
    return dict(query=query, keys=keys, values=values, grad_out=grad_out)


NEGATIVE = -1.0e30


def segment_forward(inputs):
    query_part, key_part, value_part = inputs
    factor = HD ** -0.5
    scores = jnp.dot(query_part, key_part.T, preferred_element_type=jnp.float32) * factor
    row_max = jnp.max(scores, axis=1)
    weights = jnp.exp(scores - row_max[:, None])
    row_sum = jnp.sum(weights, axis=1)
    weighted = jnp.dot(weights.astype(jnp.bfloat16), value_part, preferred_element_type=jnp.float32)
    return row_max, row_sum, weighted


def segment_backward(inputs):
    query_part, key_part, value_part, grad_part, log_part, delta_part = inputs
    factor = HD ** -0.5
    scores = jnp.dot(query_part, key_part.T, preferred_element_type=jnp.float32) * factor
    weights = jnp.exp(scores - log_part[:, None])
    grad_weights = jnp.dot(grad_part, value_part.T, preferred_element_type=jnp.float32)
    grad_scores = (weights * (grad_weights - delta_part[:, None])).astype(jnp.bfloat16)
    grad_query = jnp.dot(grad_scores, key_part, preferred_element_type=jnp.float32) * factor
    grad_keys = jnp.dot(grad_scores.T, query_part, preferred_element_type=jnp.float32) * factor
    grad_values = jnp.dot(weights.astype(jnp.bfloat16).T, grad_part, preferred_element_type=jnp.float32)
    return grad_query, grad_keys, grad_values


def kept_rows(source, stride, offset, seg_count):
    return source[offset::stride].reshape((seg_count, SEG) + source.shape[1:])


def reference(query, keys, values, grad_out):
    total_rows = query.shape[0]
    attended_cols, query_cols, key_cols, value_cols = [], [], [], []
    for head_index in range(HEADS):
        columns = slice(head_index * HD, (head_index + 1) * HD)
        head_query = query[:, columns]
        head_keys = keys[:, columns]
        head_values = values[:, columns]
        head_grad = grad_out[:, columns]
        layouts = []
        maxima, sums, accums = [], [], []
        for level_index in range(LEVELS):
            stride = 2 ** level_index
            offset = head_index % stride
            seg_count = total_rows // (SEG * stride)
            layouts.append((stride, offset, seg_count))
            level_max, level_sum, level_acc = lax.map(segment_forward, (
                kept_rows(head_query, stride, offset, seg_count),
                kept_rows(head_keys, stride, offset, seg_count),
                kept_rows(head_values, stride, offset, seg_count)))
            maxima.append(jnp.full((total_rows,), NEGATIVE, jnp.float32).at[offset::stride].set(level_max.reshape(-1)))
            sums.append(jnp.zeros((total_rows,), jnp.float32).at[offset::stride].set(level_sum.reshape(-1)))
            accums.append(jnp.zeros((total_rows, HD), jnp.float32).at[offset::stride].set(level_acc.reshape(-1, HD)))
        overall = reduce(jnp.maximum, maxima)
        denominator = jnp.zeros((total_rows,), jnp.float32)
        numerator = jnp.zeros((total_rows, HD), jnp.float32)
        for level_max, level_sum, level_acc in zip(maxima, sums, accums):
            factor_level = jnp.exp(level_max - overall)
            denominator = denominator + factor_level * level_sum
            numerator = numerator + factor_level[:, None] * level_acc
        attended = (numerator / denominator[:, None]).astype(jnp.bfloat16)
        log_total = overall + jnp.log(denominator)
        row_delta = jnp.sum(head_grad.astype(jnp.float32) * attended.astype(jnp.float32), axis=1)
        grad_query = jnp.zeros((total_rows, HD), jnp.float32)
        grad_keys = jnp.zeros((total_rows, HD), jnp.float32)
        grad_values = jnp.zeros((total_rows, HD), jnp.float32)
        for stride, offset, seg_count in layouts:
            level_query, level_keys, level_values = lax.map(segment_backward, (
                kept_rows(head_query, stride, offset, seg_count),
                kept_rows(head_keys, stride, offset, seg_count),
                kept_rows(head_values, stride, offset, seg_count),
                kept_rows(head_grad, stride, offset, seg_count),
                kept_rows(log_total, stride, offset, seg_count),
                kept_rows(row_delta, stride, offset, seg_count)))
            grad_query = grad_query.at[offset::stride].add(level_query.reshape(-1, HD))
            grad_keys = grad_keys.at[offset::stride].add(level_keys.reshape(-1, HD))
            grad_values = grad_values.at[offset::stride].add(level_values.reshape(-1, HD))
        attended_cols.append(attended)
        query_cols.append(grad_query.astype(jnp.bfloat16))
        key_cols.append(grad_keys.astype(jnp.bfloat16))
        value_cols.append(grad_values.astype(jnp.bfloat16))
    return (jnp.concatenate(attended_cols, axis=1), jnp.concatenate(query_cols, axis=1),
            jnp.concatenate(key_cols, axis=1), jnp.concatenate(value_cols, axis=1))
```

```python
import jax
import jax.numpy as jnp
from jax import lax
from jax.experimental import pallas as pl
from jax.experimental.pallas import tpu as pltpu
from jax.sharding import PartitionSpec as P

HD = 64
NEG = -1e30
F32 = jnp.float32
BF16 = jnp.bfloat16

CORE, Y_ONE, Y_TWO, Y_SIX, Z_ONE, Z_TWO = 1, 2, 4, 12, 16, 32


def swap_with(block, flip):
    count = lax.axis_size("seq")
    return lax.ppermute(block, "seq", [(i, i ^ flip) for i in range(count)])


def dot(a, b):
    return jnp.dot(a, b, preferred_element_type=F32)


def left_half(shape):
    return lax.broadcasted_iota(jnp.int32, shape, len(shape) - 1) < HD


def pair_up(first, second, odd):
    low = left_half(first.shape)
    if odd:
        return jnp.where(low, pltpu.roll(first, HD, 1), second)
    return jnp.where(low, first, pltpu.roll(second, HD, 1))


def split_heads(where_ref, q_ref, k_ref, v_ref, g_ref, send_ref, keep_ref):
    core = where_ref[0]

    def head(h):
        tile = slice((h // 2) * 128, (h // 2) * 128 + 128)
        q, k, v, g = (r[:, tile].astype(F32) for r in (q_ref, k_ref, v_ref, g_ref))
        return pair_up(q, g, h % 2), pair_up(k, v, h % 2)

    for s in range(3):
        low, high = head(s), head(s + 3)
        for part in range(2):
            cols = slice(s * 256 + part * 128, s * 256 + part * 128 + 128)
            keep_ref[:, cols] = jnp.where(core == 0, low[part], high[part]).astype(BF16)
            send_ref[:, cols] = jnp.where(core == 0, high[part], low[part]).astype(BF16)


def source_rows(shape, axis, head):
    i = lax.broadcasted_iota(jnp.int32, shape, axis)
    row = jnp.where(i < 64, 4 + 8 * (i - 32), jnp.where(i < 128, 2 + 4 * (i - 64), 1 + 2 * (i - 128)))
    row = jnp.where(i < 16, 16 * i, jnp.where(i < 32, 8 + 16 * (i - 16), row))
    return (row + head) & 255


def sort_rows(where_ref, keep_ref, recv_ref, send_ref, own_ref):
    core, odd = where_ref[0], where_ref[1]
    keep, recv = keep_ref[...], recv_ref[...]
    rows = jnp.concatenate(
        [jnp.where(core == 0, keep, recv), jnp.where(core == 0, recv, keep)], 0
    )
    lane = lax.broadcasted_iota(jnp.int32, (256, 256), 1)
    slots = []
    for s in range(3):
        order = (lane == source_rows((256, 256), 0, 3 * core + s)).astype(BF16)
        slots.append(dot(order, rows[:, s * 256 : s * 256 + 256]))
    send_ref[:, :256] = jnp.where(odd == 0, slots[2], slots[0]).astype(BF16)
    send_ref[:, 256:] = slots[1][:, 128:].astype(BF16)
    own_ref[:, :256] = jnp.where(odd == 0, slots[0], slots[2]).astype(BF16)
    own_ref[:, 256:] = slots[1].astype(BF16)


def unsort_rows(where_ref, own_ref, recv_ref, send_ref, keep_ref):
    core, odd = where_ref[0], where_ref[1]
    first = jnp.where(odd == 0, own_ref[:, :256], recv_ref[:, :256].astype(F32)).astype(BF16)
    third = jnp.where(odd == 0, recv_ref[:, :256].astype(F32), own_ref[:, :256]).astype(BF16)
    middle = jnp.concatenate(
        [own_ref[:, 256:384], own_ref[:, 384:] + recv_ref[:, 256:].astype(F32)], 1
    ).astype(BF16)
    sub = lax.broadcasted_iota(jnp.int32, (256, 256), 0)
    for s, slot in enumerate((first, middle, third)):
        order = (sub == source_rows((256, 256), 1, 3 * core + s)).astype(BF16)
        rows = dot(order, slot)
        cols = slice(s * 256, s * 256 + 256)
        keep_ref[:, cols] = jnp.where(core == 0, rows[:128], rows[128:]).astype(BF16)
        send_ref[:, cols] = jnp.where(core == 0, rows[128:], rows[:128]).astype(BF16)


def join_heads(where_ref, keep_ref, recv_ref, att_ref, dq_ref, dk_ref, dv_ref):
    core = where_ref[0]
    keep, recv = keep_ref[...].astype(F32), recv_ref[...].astype(F32)
    low = jnp.where(core == 0, keep, recv)
    high = jnp.where(core == 0, recv, keep)

    def part(h, p):
        half = low if h < 3 else high
        start = (h % 3) * 256 + p * 128
        return half[:, start : start + 128]

    mask = left_half((128, 128))
    for p, (left_ref, right_ref) in enumerate(((dq_ref, att_ref), (dk_ref, dv_ref))):
        for j in range(3):
            even, odd = part(2 * j, p), part(2 * j + 1, p)
            tile = slice(j * 128, j * 128 + 128)
            left_ref[:, tile] = jnp.where(mask, even, pltpu.roll(odd, HD, 1)).astype(BF16)
            right_ref[:, tile] = jnp.where(mask, pltpu.roll(even, HD, 1), odd).astype(BF16)


def rank(shape, axis, step):
    i = lax.broadcasted_iota(jnp.int32, shape, axis)
    rank_of = jnp.zeros(shape, F32)
    for level in range(4):
        rank_of = rank_of + (i < (step << level)).astype(F32)
    return rank_of


def key_rank(part, shape):
    i = lax.broadcasted_iota(jnp.int32, shape, 0)
    if part == 2:
        i = i & 127
    elif part == 3:
        i = i & 63
    elif part == 4:
        i = i & 31
    rank_of = jnp.zeros(shape, F32)
    for level in range(4):
        rank_of = rank_of + (i < (32 << level)).astype(F32)
    return rank_of


def attend(qga_ref, qgb_ref, kv0_ref, r1_ref, r2_ref, r3_ref, r4_ref,
           outa_ref, outb_ref, d0_ref, d1_ref, d2_ref, d3_ref, d4_ref, e_ref):
    kv_refs = (kv0_ref, r1_ref, r2_ref, r3_ref, r4_ref)
    d_refs = (d0_ref, d1_ref, d2_ref, d3_ref, d4_ref)
    sub = lax.broadcasted_iota(jnp.int32, (128, 1), 0) < HD
    for which, (qg_ref, out_ref) in enumerate(((qga_ref, outa_ref), (qgb_ref, outb_ref))):
        cols = slice(which * 128, which * 128 + 128)
        total = qg_ref.shape[0]
        step = total // 16
        qg = qg_ref[...].astype(F32)
        scaled = jnp.where(left_half(qg.shape), qg * HD**-0.5, qg)
        qg_b = scaled.astype(BF16)
        turned = scaled.T
        q_t = jnp.where(sub, turned, 0.0).astype(BF16)
        g_t = jnp.where(sub, 0.0, turned)
        g_tb = g_t.astype(BF16)
        half = total // 2
        pieces = [(0, 0, 256, 0, half, True), (0, 0, 256, half, half, False), (0, 256, 256, 0, total, False)]
        for part in range(1, 5):
            pieces.append((part, 0, 256, 0, max(128, total >> part), True))
        maxima = [jnp.full((1, 128), NEG, F32) for _ in range(total // 128)]
        place = 0
        places, counts = [], []
        for part, row, rows, first, width, weighted in pieces:
            keys = kv_refs[part][row : row + rows, cols]
            scores = dot(keys, q_t[:, first : first + width])
            count = None
            if weighted:
                count = jnp.minimum(key_rank(part, (rows, width)), rank((rows, width), 1, step)) + (1.0 - part)
                if part > 0 and (total >> part) < width:
                    scores = jnp.where(count > 0.0, scores, NEG)
                count = jnp.maximum(count, 0.0)
            e_ref[place : place + rows, :width] = scores
            top = jnp.max(scores, axis=0, keepdims=True)
            for t in range(width // 128):
                at = first // 128 + t
                maxima[at] = jnp.maximum(maxima[at], top[:, t * 128 : t * 128 + 128])
            places.append(place)
            counts.append(count)
            place += rows
        peak = jnp.concatenate(maxima, 1)
        sums = [jnp.zeros((1, 128), F32) for _ in range(total // 128)]
        accs = [jnp.zeros((128, 128), F32) for _ in range(total // 128)]
        for (part, row, rows, first, width, weighted), place, count in zip(pieces, places, counts):
            weights = jnp.exp(e_ref[place : place + rows, :width] - peak[:, first : first + width])
            if weighted:
                weights = weights * count
            e_ref[place : place + rows, :width] = weights
            turned_keys = kv_refs[part][row : row + rows, cols].T
            acc = dot(turned_keys, weights.astype(BF16))
            total_w = jnp.sum(weights, axis=0, keepdims=True)
            for t in range(width // 128):
                at = first // 128 + t
                sums[at] = sums[at] + total_w[:, t * 128 : t * 128 + 128]
                accs[at] = accs[at] + acc[:, t * 128 : t * 128 + 128]
        inverse = 1.0 / jnp.concatenate(sums, 1)
        attended = (jnp.concatenate(accs, 1) * inverse).astype(BF16).astype(F32)
        delta = jnp.sum(g_t * attended, axis=0, keepdims=True)
        queries = [jnp.zeros((128, 128), F32) for _ in range(total // 128)]
        partial = {}
        for (part, row, rows, first, width, weighted), place in zip(pieces, places):
            span = slice(first, first + width)
            keys = kv_refs[part][row : row + rows, cols]
            probs = e_ref[place : place + rows, :width] * inverse[:, span]
            grads = probs * (dot(keys, g_tb[:, span]) - delta[:, span])
            grads_b = grads.astype(BF16)
            d_keys = dot(grads_b, qg_b[span])
            d_vals = dot(probs.astype(BF16), qg_b[span])
            both = jnp.where(left_half(d_keys.shape), d_keys, d_vals)
            if (part, row) in partial:
                both = both + partial[part, row]
            partial[part, row] = both
            d_query = dot(keys.T, grads_b)
            for t in range(width // 128):
                at = first // 128 + t
                queries[at] = queries[at] + d_query[:, t * 128 : t * 128 + 128]
        for (part, row), both in partial.items():
            ref = d_refs[part]
            ref[row : row + 256, cols] = both.astype(ref.dtype)
        out = jnp.where(sub, jnp.concatenate(queries, 1) * HD**-0.5, attended)
        out_ref[...] = out.T


def call(body, outs, *args, scalar=True, scratch=(), flops=0):
    vmem = pl.BlockSpec(memory_space=pltpu.VMEM)
    specs = [vmem] * len(args)
    if scalar:
        specs[0] = pl.BlockSpec(memory_space=pltpu.SMEM)
    moved = sum(a.size * a.dtype.itemsize for a in args)
    return pl.pallas_call(
        body,
        out_shape=[jax.ShapeDtypeStruct(s, d) for s, d in outs],
        in_specs=specs,
        out_specs=[vmem] * len(outs),
        scratch_shapes=list(scratch),
        compiler_params=pltpu.CompilerParams(vmem_limit_bytes=48 * 1024 * 1024),
        cost_estimate=pl.CostEstimate(flops=flops, bytes_accessed=moved, transcendentals=0),
    )(*args)


CLASSES = (0, 16, 32, 64, 128, 256)


def interleave(own, partner):
    parts = []
    for a, b in zip(CLASSES, CLASSES[1:]):
        parts += [own[a:b], partner[a:b]]
    return jnp.concatenate(parts, 0)


def separate(rows):
    own, partner = [], []
    for a, b in zip(CLASSES, CLASSES[1:]):
        own.append(rows[2 * a : a + b])
        partner.append(rows[a + b : 2 * b])
    return jnp.concatenate(own, 0), jnp.concatenate(partner, 0)


def head_rows(blocks, rows):
    return jnp.concatenate([array[at : at + rows] for array, at in blocks], 0)


def add_rows(arrays, blocks, rows, extra):
    extra = extra.astype(F32)
    for n, (name, at) in enumerate(blocks):
        piece = extra[n * rows : n * rows + rows]
        arrays[name] = lax.dynamic_update_slice_in_dim(
            arrays[name], arrays[name][at : at + rows] + piece, at, 0
        )


def per_device(query, keys, values, grad_out):
    device = lax.axis_index("seq")
    place = jnp.stack([device & 1, (device >> 1) & 1]).astype(jnp.int32)
    send, keep = call(split_heads, [((128, 768), BF16)] * 2, place, query, keys, values, grad_out)
    send, own = call(sort_rows, [((256, 384), BF16), ((256, 512), BF16)], place, keep, swap_with(send, CORE))
    other = swap_with(send, Y_ONE)
    qg_a = interleave(own[:, :128], other[:, :128])
    qg_b = own[:, 256:384]
    kv0 = interleave(
        jnp.concatenate([own[:, 128:256], own[:, 384:]], 1), other[:, 128:]
    )
    b1 = [(0, 0)]
    b2 = b1 + [(1, 0)]
    b3 = b2 + [(2, 0), (2, 128)]
    b4 = b3 + [(3, 0), (3, 64), (3, 128), (3, 192)]
    steps = ((b1, 256, Y_TWO), (b2, 128, Y_SIX), (b3, 64, Z_ONE), (b4, 32, Z_TWO))
    kv = [kv0]
    for blocks, rows, flip in steps:
        kv.append(swap_with(head_rows([(kv[n], at) for n, at in blocks], rows), flip))
    out_a, out_b, *grads = call(
        attend,
        [((512, 128), F32), ((256, 128), F32), ((512, 256), F32)]
        + [((256, 256), F32)] * 3 + [((256, 256), BF16)],
        qg_a, qg_b, *kv,
        scalar=False,
        scratch=[pltpu.VMEM((7 * 256, 512), F32)],
        flops=int(6e8),
    )
    for part, (blocks, rows, flip) in reversed(list(enumerate(steps, 1))):
        add_rows(grads, blocks, rows, swap_with(grads[part].astype(BF16), flip))
    own_a, other_a = separate(out_a)
    own_kv, other_kv = separate(grads[0])
    send = jnp.concatenate([other_a, other_kv], 1).astype(BF16)
    own = jnp.concatenate([own_a, own_kv[:, :128], out_b, own_kv[:, 128:]], 1)
    send, keep = call(unsort_rows, [((128, 768), BF16)] * 2, place, own, swap_with(send, Y_ONE))
    return tuple(
        call(join_heads, [((128, 384), BF16)] * 4, place, keep, swap_with(send, CORE))
    )


def solution(mesh):
    spec = P("seq", None)
    return jax.shard_map(
        per_device, mesh=mesh, in_specs=(spec,) * 4, out_specs=(spec,) * 4, check_vma=False
    )
```

```python
import jax
import jax.numpy as jnp
from jax import lax
from jax.experimental import pallas as pl
from jax.experimental.pallas import tpu as pltpu
from jax.sharding import PartitionSpec as P

HD = 64
NEG = -1e30
F32 = jnp.float32
BF16 = jnp.bfloat16

CORE, Y_ONE, Y_TWO, Y_SIX, Z_ONE, Z_TWO = 1, 2, 4, 12, 16, 32


def gather_pair(block, flip):
    count = lax.axis_size("seq")
    pairs = [[i, i ^ flip] for i in range(count) if i < i ^ flip]
    return lax.all_gather(block, "seq", axis_index_groups=pairs, axis=0, tiled=False)


def swap_with(block, flip):
    both = gather_pair(block, flip)
    high = 1 << (flip.bit_length() - 1)
    first = (lax.axis_index("seq") & high) == 0
    return jnp.where(first, both[1], both[0])


def dot(a, b):
    return jnp.dot(a, b, preferred_element_type=F32)


def left_half(shape):
    return lax.broadcasted_iota(jnp.int32, shape, len(shape) - 1) < HD


def pair_up(first, second, odd):
    low = left_half(first.shape)
    if odd:
        return jnp.where(low, pltpu.roll(first, HD, 1), second)
    return jnp.where(low, first, pltpu.roll(second, HD, 1))


def source_rows(shape, axis, head):
    i = lax.broadcasted_iota(jnp.int32, shape, axis)
    row = jnp.where(i < 64, 4 + 8 * (i - 32), jnp.where(i < 128, 2 + 4 * (i - 64), 1 + 2 * (i - 128)))
    row = jnp.where(i < 16, 16 * i, jnp.where(i < 32, 8 + 16 * (i - 16), row))
    return (row + head) & 255


def sort_rows(where_ref, x_ref, send_ref, own_ref):
    core, odd = where_ref[0], where_ref[1]

    def tile(array, h):
        cols = slice((h // 2) * 128, (h // 2) * 128 + 128)
        return jnp.concatenate([x_ref[0, array, :, cols], x_ref[1, array, :, cols]], 0).astype(F32)

    def head(h):
        q, k, v, g = (tile(array, h) for array in range(4))
        return jnp.concatenate([pair_up(q, g, h % 2), pair_up(k, v, h % 2)], 1)

    lane = lax.broadcasted_iota(jnp.int32, (256, 256), 1)
    slots = []
    for s in range(3):
        rows = jnp.where(core == 0, head(s), head(s + 3)).astype(BF16)
        order = (lane == source_rows((256, 256), 0, 3 * core + s)).astype(BF16)
        slots.append(dot(order, rows))
    send_ref[:, :256] = jnp.where(odd == 0, slots[2], slots[0]).astype(BF16)
    send_ref[:, 256:] = slots[1][:, 128:].astype(BF16)
    own_ref[:, :256] = jnp.where(odd == 0, slots[0], slots[2]).astype(BF16)
    own_ref[:, 256:] = slots[1].astype(BF16)


def unsort_rows(where_ref, own_ref, recv_ref, send_ref, keep_ref):
    core, odd = where_ref[0], where_ref[1]
    first = jnp.where(odd == 0, own_ref[:, :256], recv_ref[:, :256].astype(F32)).astype(BF16)
    third = jnp.where(odd == 0, recv_ref[:, :256].astype(F32), own_ref[:, :256]).astype(BF16)
    middle = jnp.concatenate(
        [own_ref[:, 256:384], own_ref[:, 384:] + recv_ref[:, 256:].astype(F32)], 1
    ).astype(BF16)
    sub = lax.broadcasted_iota(jnp.int32, (256, 256), 0)
    for s, slot in enumerate((first, middle, third)):
        order = (sub == source_rows((256, 256), 1, 3 * core + s)).astype(BF16)
        rows = dot(order, slot)
        cols = slice(s * 256, s * 256 + 256)
        keep_ref[:, cols] = jnp.where(core == 0, rows[:128], rows[128:]).astype(BF16)
        send_ref[:, cols] = jnp.where(core == 0, rows[128:], rows[:128]).astype(BF16)


def join_heads(where_ref, keep_ref, recv_ref, att_ref, dq_ref, dk_ref, dv_ref):
    core = where_ref[0]
    keep, recv = keep_ref[...].astype(F32), recv_ref[1 - core].astype(F32)
    low = jnp.where(core == 0, keep, recv)
    high = jnp.where(core == 0, recv, keep)

    def part(h, p):
        half = low if h < 3 else high
        start = (h % 3) * 256 + p * 128
        return half[:, start : start + 128]

    mask = left_half((128, 128))
    for p, (left_ref, right_ref) in enumerate(((dq_ref, att_ref), (dk_ref, dv_ref))):
        for j in range(3):
            even, odd = part(2 * j, p), part(2 * j + 1, p)
            tile = slice(j * 128, j * 128 + 128)
            left_ref[:, tile] = jnp.where(mask, even, pltpu.roll(odd, HD, 1)).astype(BF16)
            right_ref[:, tile] = jnp.where(mask, pltpu.roll(even, HD, 1), odd).astype(BF16)


def rank(shape, axis, step):
    i = lax.broadcasted_iota(jnp.int32, shape, axis)
    rank_of = jnp.zeros(shape, F32)
    for level in range(4):
        rank_of = rank_of + (i < (step << level)).astype(F32)
    return rank_of


def levels_shared(level, shape, step):
    i = lax.broadcasted_iota(jnp.int32, shape, 0)
    i = i & (511 >> level)
    key = jnp.zeros(shape, F32)
    for k in range(4):
        key = key + (i < (32 << k)).astype(F32)
    return jnp.maximum(jnp.minimum(key, rank(shape, 1, step)) + (1.0 - level), 0.0)


def attend(qga_ref, qgb_ref, kv0_ref, r1_ref, r2_ref, r3_ref, r4_ref,
           outa_ref, outb_ref, d0_ref, d1_ref, d2_ref, d3_ref, d4_ref, e_ref):
    kv_refs = (kv0_ref, r1_ref, r2_ref, r3_ref, r4_ref)
    d_refs = (d0_ref, d1_ref, d2_ref, d3_ref, d4_ref)
    sub = lax.broadcasted_iota(jnp.int32, (128, 1), 0) < HD
    for which, (qg_ref, out_ref) in enumerate(((qga_ref, outa_ref), (qgb_ref, outb_ref))):
        cols = slice(which * 128, which * 128 + 128)
        total = qg_ref.shape[0]
        step = total // 16
        qg = qg_ref[...].astype(F32)
        scaled = jnp.where(left_half(qg.shape), qg * HD**-0.5, qg)
        qg_b = scaled.astype(BF16)
        turned = scaled.T
        q_t = jnp.where(sub, turned, 0.0).astype(BF16)
        g_t = jnp.where(sub, 0.0, turned)
        g_tb = g_t.astype(BF16)
        half = total // 2
        pieces = [(0, 0, 256, 0, half, 0), (0, 0, 256, half, half, None), (0, 256, 256, 0, total, None)]
        for part, row, rows, level in ((1, 0, 256, 1), (2, 0, 256, 2), (3, 0, 256, 3), (3, 256, 128, 4), (4, 0, 128, 4)):
            pieces.append((part, row, rows, 0, max(128, total >> level), level))
        maxima = [jnp.full((1, 128), NEG, F32) for _ in range(total // 128)]
        place = 0
        places, counts = [], []
        for part, row, rows, first, width, level in pieces:
            keys = kv_refs[part][row : row + rows, cols]
            scores = dot(keys, q_t[:, first : first + width])
            count = None
            if level is not None:
                count = levels_shared(level, (rows, width), step)
                if total >> level < width:
                    scores = jnp.where(count > 0.0, scores, NEG)
            e_ref[place : place + rows, :width] = scores
            top = jnp.max(scores, axis=0, keepdims=True)
            for t in range(width // 128):
                at = first // 128 + t
                maxima[at] = jnp.maximum(maxima[at], top[:, t * 128 : t * 128 + 128])
            places.append(place)
            counts.append(count)
            place += rows
        peak = jnp.concatenate(maxima, 1)
        sums = [jnp.zeros((1, 128), F32) for _ in range(total // 128)]
        accs = [jnp.zeros((128, 128), F32) for _ in range(total // 128)]
        for (part, row, rows, first, width, level), place, count in zip(pieces, places, counts):
            weights = jnp.exp(e_ref[place : place + rows, :width] - peak[:, first : first + width])
            if level is not None:
                weights = weights * count
            e_ref[place : place + rows, :width] = weights
            turned_keys = kv_refs[part][row : row + rows, cols].T
            acc = dot(turned_keys, weights.astype(BF16))
            total_w = jnp.sum(weights, axis=0, keepdims=True)
            for t in range(width // 128):
                at = first // 128 + t
                sums[at] = sums[at] + total_w[:, t * 128 : t * 128 + 128]
                accs[at] = accs[at] + acc[:, t * 128 : t * 128 + 128]
        inverse = 1.0 / jnp.concatenate(sums, 1)
        attended = (jnp.concatenate(accs, 1) * inverse).astype(BF16).astype(F32)
        delta = jnp.sum(g_t * attended, axis=0, keepdims=True)
        queries = [jnp.zeros((128, 128), F32) for _ in range(total // 128)]
        partial = {}
        for (part, row, rows, first, width, level), place in zip(pieces, places):
            span = slice(first, first + width)
            keys = kv_refs[part][row : row + rows, cols]
            probs = e_ref[place : place + rows, :width] * inverse[:, span]
            grads = probs * (dot(keys, g_tb[:, span]) - delta[:, span])
            grads_b = grads.astype(BF16)
            d_keys = dot(grads_b, qg_b[span])
            d_vals = dot(probs.astype(BF16), qg_b[span])
            both = jnp.where(left_half(d_keys.shape), d_keys, d_vals)
            if (part, row) in partial:
                both = both + partial[part, row]
            partial[part, row] = both
            d_query = dot(keys.T, grads_b)
            for t in range(width // 128):
                at = first // 128 + t
                queries[at] = queries[at] + d_query[:, t * 128 : t * 128 + 128]
        for (part, row), both in partial.items():
            ref = d_refs[part]
            ref[row : row + both.shape[0], cols] = both.astype(ref.dtype)
        out = jnp.where(sub, jnp.concatenate(queries, 1) * HD**-0.5, attended)
        out_ref[...] = out.T


def call(body, outs, *args, scalar=True, scratch=(), flops=0):
    vmem = pl.BlockSpec(memory_space=pltpu.VMEM)
    specs = [vmem] * len(args)
    if scalar:
        specs[0] = pl.BlockSpec(memory_space=pltpu.SMEM)
    moved = sum(a.size * a.dtype.itemsize for a in args)
    return pl.pallas_call(
        body,
        out_shape=[jax.ShapeDtypeStruct(s, d) for s, d in outs],
        in_specs=specs,
        out_specs=[vmem] * len(outs),
        scratch_shapes=list(scratch),
        compiler_params=pltpu.CompilerParams(vmem_limit_bytes=48 * 1024 * 1024),
        cost_estimate=pl.CostEstimate(flops=flops, bytes_accessed=moved, transcendentals=0),
    )(*args)


CLASSES = (0, 16, 32, 64, 128, 256)


def interleave(own, partner):
    parts = []
    for a, b in zip(CLASSES, CLASSES[1:]):
        parts += [own[a:b], partner[a:b]]
    return jnp.concatenate(parts, 0)


def separate(rows):
    own, partner = [], []
    for a, b in zip(CLASSES, CLASSES[1:]):
        own.append(rows[2 * a : a + b])
        partner.append(rows[a + b : 2 * b])
    return jnp.concatenate(own, 0), jnp.concatenate(partner, 0)


def add_rows(arrays, blocks, extra):
    extra, start = extra.astype(F32), 0
    for n, at, size in blocks:
        piece = arrays[n][at : at + size] + extra[start : start + size]
        arrays[n] = lax.dynamic_update_slice_in_dim(arrays[n], piece, at, 0)
        start += size


def per_device(query, keys, values, grad_out):
    device = lax.axis_index("seq")
    place = jnp.stack([device & 1, (device >> 1) & 1]).astype(jnp.int32)
    chip_rows = gather_pair(jnp.stack([query, keys, values, grad_out]), CORE)
    send, own = call(sort_rows, [((256, 384), BF16), ((256, 512), BF16)], place, chip_rows)
    other = swap_with(send, Y_ONE)
    qg_a = interleave(own[:, :128], other[:, :128])
    qg_b = own[:, 256:384]
    kv0 = interleave(
        jnp.concatenate([own[:, 128:256], own[:, 384:]], 1), other[:, 128:]
    )
    b1 = [(0, 0, 256)]
    b2 = [(0, 0, 128), (1, 0, 128)]
    ring = [(0, 0), (1, 0), (2, 0), (2, 128)]
    b4 = [(n, at, 32) for n, at in ring]
    b3 = [(n, at, 64) for n, at in ring] + [(4, 0, 128)]
    steps = ((1, b1, Y_TWO), (2, b2, Y_SIX), (4, b4, Z_TWO), (3, b3, Z_ONE))
    kv = {0: kv0}
    for part, blocks, flip in steps:
        rows = jnp.concatenate([kv[n][at : at + size] for n, at, size in blocks], 0)
        kv[part] = swap_with(rows, flip)
    out_a, out_b, *grads = call(
        attend,
        [((512, 128), F32), ((256, 128), F32), ((512, 256), F32)]
        + [((n, 256), F32) for n in (256, 256, 384, 128)],
        qg_a, qg_b, *(kv[n] for n in range(5)),
        scalar=False,
        scratch=[pltpu.VMEM((7 * 256, 512), F32)],
        flops=int(6e8),
    )
    for part, blocks, flip in reversed(steps):
        add_rows(grads, blocks, swap_with(grads[part].astype(BF16), flip))
    own_a, other_a = separate(out_a)
    own_kv, other_kv = separate(grads[0])
    send = jnp.concatenate([other_a, other_kv], 1).astype(BF16)
    own = jnp.concatenate([own_a, own_kv[:, :128], out_b, own_kv[:, 128:]], 1)
    send, keep = call(unsort_rows, [((128, 768), BF16)] * 2, place, own, swap_with(send, Y_ONE))
    return tuple(
        call(join_heads, [((128, 384), BF16)] * 4, place, keep, gather_pair(send, CORE))
    )


def solution(mesh):
    spec = P("seq", None)
    return jax.shard_map(
        per_device, mesh=mesh, in_specs=(spec,) * 4, out_specs=(spec,) * 4, check_vma=False
    )
```

```python
import jax
import jax.numpy as jnp
from jax import lax
from jax.experimental import pallas as pl
from jax.experimental.pallas import tpu as pltpu
from jax.sharding import PartitionSpec as P

HD = 64
NEG = -1e30
F32 = jnp.float32
BF16 = jnp.bfloat16

CORE, Y_ONE, Y_THREE, Y_SIX, Z_ONE, Z_TWO = 1, 2, 6, 12, 16, 32


def gather_pair(block, flip):
    count = lax.axis_size("seq")
    pairs = [[i, i ^ flip] for i in range(count) if i < i ^ flip]
    return lax.all_gather(block, "seq", axis_index_groups=pairs, axis=0, tiled=False)


def swap_with(block, flip):
    both = gather_pair(block, flip)
    high = 1 << (flip.bit_length() - 1)
    first = (lax.axis_index("seq") & high) == 0
    return jnp.where(first, both[1], both[0])


def dot(a, b):
    return jnp.dot(a, b, preferred_element_type=F32)


def left_half(shape):
    return lax.broadcasted_iota(jnp.int32, shape, len(shape) - 1) < HD


def pair_up(first, second, odd):
    low = left_half(first.shape)
    if odd:
        return jnp.where(low, pltpu.roll(first, HD, 1), second)
    return jnp.where(low, first, pltpu.roll(second, HD, 1))


def source_rows(shape, axis, head):
    i = lax.broadcasted_iota(jnp.int32, shape, axis)
    row = jnp.where(i < 64, 4 + 8 * (i - 32), jnp.where(i < 128, 2 + 4 * (i - 64), 1 + 2 * (i - 128)))
    row = jnp.where(i < 16, 16 * i, jnp.where(i < 32, 8 + 16 * (i - 16), row))
    return (row + head) & 255


def sort_rows(where_ref, x_ref, send_ref, own_ref):
    core, odd = where_ref[0], where_ref[1]

    def tile(array, h):
        cols = slice((h // 2) * 128, (h // 2) * 128 + 128)
        return jnp.concatenate([x_ref[0, array, :, cols], x_ref[1, array, :, cols]], 0).astype(F32)

    def head(h):
        q, k, v, g = (tile(array, h) for array in range(4))
        return jnp.concatenate([pair_up(q, g, h % 2), pair_up(k, v, h % 2)], 1)

    lane = lax.broadcasted_iota(jnp.int32, (256, 256), 1)
    slots = []
    for s in range(3):
        rows = jnp.where(core == 0, head(s), head(s + 3)).astype(BF16)
        order = (lane == source_rows((256, 256), 0, 3 * core + s)).astype(BF16)
        slots.append(dot(order, rows))
    send_ref[:, :256] = jnp.where(odd == 0, slots[2], slots[0]).astype(BF16)
    send_ref[:, 256:] = slots[1][:, 128:].astype(BF16)
    own_ref[:, :256] = jnp.where(odd == 0, slots[0], slots[2]).astype(BF16)
    own_ref[:, 256:] = slots[1].astype(BF16)


def unsort_rows(where_ref, own_ref, recv_ref, send_ref, keep_ref):
    core, odd = where_ref[0], where_ref[1]
    first = jnp.where(odd == 0, own_ref[:, :256], recv_ref[:, :256].astype(F32)).astype(BF16)
    third = jnp.where(odd == 0, recv_ref[:, :256].astype(F32), own_ref[:, :256]).astype(BF16)
    middle = jnp.concatenate(
        [own_ref[:, 256:384], own_ref[:, 384:] + recv_ref[:, 256:].astype(F32)], 1
    ).astype(BF16)
    sub = lax.broadcasted_iota(jnp.int32, (256, 256), 0)
    for s, slot in enumerate((first, middle, third)):
        order = (sub == source_rows((256, 256), 1, 3 * core + s)).astype(BF16)
        rows = dot(order, slot)
        cols = slice(s * 256, s * 256 + 256)
        keep_ref[:, cols] = jnp.where(core == 0, rows[:128], rows[128:]).astype(BF16)
        send_ref[:, cols] = jnp.where(core == 0, rows[128:], rows[:128]).astype(BF16)


def join_heads(where_ref, keep_ref, recv_ref, att_ref, dq_ref, dk_ref, dv_ref):
    core = where_ref[0]
    keep, recv = keep_ref[...].astype(F32), recv_ref[1 - core].astype(F32)
    low = jnp.where(core == 0, keep, recv)
    high = jnp.where(core == 0, recv, keep)

    def part(h, p):
        half = low if h < 3 else high
        start = (h % 3) * 256 + p * 128
        return half[:, start : start + 128]

    mask = left_half((128, 128))
    for p, (left_ref, right_ref) in enumerate(((dq_ref, att_ref), (dk_ref, dv_ref))):
        for j in range(3):
            even, odd = part(2 * j, p), part(2 * j + 1, p)
            tile = slice(j * 128, j * 128 + 128)
            left_ref[:, tile] = jnp.where(mask, even, pltpu.roll(odd, HD, 1)).astype(BF16)
            right_ref[:, tile] = jnp.where(mask, pltpu.roll(even, HD, 1), odd).astype(BF16)


PIECES = ((0, 0, 256, 0), (0, 256, 256, None), (1, 0, 256, 1), (2, 0, 256, 2), (3, 0, 256, 3), (3, 256, 128, 4), (4, 0, 128, 4))
STARTS = (0, 512, 768, 1024, 1408)


def rank(shape, axis, step):
    i = lax.broadcasted_iota(jnp.int32, shape, axis)
    return sum((i < (step << level)).astype(F32) for level in range(4))


def key_ranks(level):
    i = lax.broadcasted_iota(jnp.int32, (256, 128), 0) & (511 >> max(level, 1))
    return sum((i < (32 << k)).astype(F32) for k in range(4))


def attend(qga_ref, qgb_ref, kv0_ref, r1_ref, r2_ref, r3_ref, r4_ref,
           outa_ref, outb_ref, d0_ref, d1_ref, d2_ref, d3_ref, d4_ref,
           ea_ref, eb_ref, pa_ref, pb_ref, ta_ref, tb_ref):
    kv_refs = (kv0_ref, r1_ref, r2_ref, r3_ref, r4_ref)
    d_refs = (d0_ref, d1_ref, d2_ref, d3_ref, d4_ref)
    sub = lax.broadcasted_iota(jnp.int32, (128, 1), 0) < HD
    ranks = [key_ranks(level) for level in (1, 2, 3)]
    heads = []
    for which, (qg_ref, out_ref, e_ref, p_ref, t_ref) in enumerate(
        ((qga_ref, outa_ref, ea_ref, pa_ref, ta_ref), (qgb_ref, outb_ref, eb_ref, pb_ref, tb_ref))
    ):
        total = qg_ref.shape[0]
        qg = qg_ref[...].astype(F32)
        low = left_half(qg.shape)
        turned = qg.T
        g_t = jnp.where(sub, 0.0, turned)
        query_rank = rank((1, 128), 1, total // 16)
        shared = [jnp.minimum(r, query_rank) for r in ranks]
        head = dict(
            total=total, out=out_ref, e=e_ref, p=p_ref, t=t_ref, g_t=g_t, g_tb=g_t.astype(BF16),
            q_t=jnp.where(sub, turned * HD**-0.5, 0.0).astype(BF16),
            q_b=jnp.where(low, qg * HD**-0.5, 0.0).astype(BF16),
            g_b=jnp.where(low, 0.0, qg).astype(BF16),
            cols=slice(which * 128, which * 128 + 128), pieces=[],
        )
        place = 0
        for part, row, rows, level in PIECES:
            width = max(128, total >> (level or 0))
            counts = [None] * (width // 128)
            if level is not None and level < 4:
                counts[0] = shared[max(level, 1) - 1] + (1.0 - level)
            if level == 0 and total == 512:
                counts[1] = 2.0
            valid = None
            if level is not None and total >> level < 128:
                valid = query_rank >= level
            head["pieces"].append((part, row, rows, width, place, counts, valid))
            place += rows
        heads.append(head)

    for head in heads:
        head["top"] = [jnp.full((1, 128), NEG, F32) for _ in range(head["total"] // 128)]
    for n in range(len(PIECES)):
        for head in heads:
            part, row, rows, width, place, counts, valid = head["pieces"][n]
            keys = kv_refs[part][row : row + rows, head["cols"]]
            start = STARTS[part] + row
            head["t"][:, start : start + rows] = keys.T
            scores = dot(keys, head["q_t"][:, :width])
            head["p"][place : place + rows, :width] = dot(keys, head["g_tb"][:, :width])
            if valid is not None:
                scores = jnp.where(valid, scores, NEG)
            head["e"][place : place + rows, :width] = scores
            top = jnp.max(scores, axis=0, keepdims=True)
            for t in range(width // 128):
                head["top"][t] = jnp.maximum(head["top"][t], top[:, t * 128 : t * 128 + 128])

    for head in heads:
        tiles = head["total"] // 128
        head["peak"] = jnp.concatenate(head["top"], 1)
        head["sums"] = [jnp.zeros((1, 128), F32) for _ in range(tiles)]
        head["accs"] = [jnp.zeros((128, 128), F32) for _ in range(tiles)]
    for n in range(len(PIECES)):
        for head in heads:
            part, row, rows, width, place, counts, valid = head["pieces"][n]
            weights = jnp.exp(head["e"][place : place + rows, :width] - head["peak"][:, :width])
            if any(count is not None for count in counts):
                cut = [weights[:, t * 128 : t * 128 + 128] for t in range(width // 128)]
                cut = [w if c is None else w * c for w, c in zip(cut, counts)]
                weights = jnp.concatenate(cut, 1)
            head["e"][place : place + rows, :width] = weights
            start = STARTS[part] + row
            acc = dot(head["t"][:, start : start + rows], weights.astype(BF16))
            added = jnp.sum(weights, axis=0, keepdims=True)
            for t in range(width // 128):
                tile = slice(t * 128, t * 128 + 128)
                head["sums"][t] = head["sums"][t] + added[:, tile]
                head["accs"][t] = head["accs"][t] + acc[:, tile]

    for head in heads:
        head["inverse"] = 1.0 / jnp.concatenate(head["sums"], 1)
        head["att"] = (jnp.concatenate(head["accs"], 1) * head["inverse"]).astype(BF16).astype(F32)
        head["delta"] = jnp.sum(head["g_t"] * head["att"], axis=0, keepdims=True)
        head["grads"] = [jnp.zeros((128, 128), F32) for _ in range(head["total"] // 128)]
    for n in range(len(PIECES)):
        for head in heads:
            part, row, rows, width, place, counts, valid = head["pieces"][n]
            probs = head["e"][place : place + rows, :width] * head["inverse"][:, :width]
            grads = probs * (head["p"][place : place + rows, :width] - head["delta"][:, :width])
            grads = grads.astype(BF16)
            both = dot(grads, head["q_b"][:width]) + dot(probs.astype(BF16), head["g_b"][:width])
            d_refs[part][row : row + rows, head["cols"]] = both
            start = STARTS[part] + row
            d_query = dot(head["t"][:, start : start + rows], grads)
            for t in range(width // 128):
                head["grads"][t] = head["grads"][t] + d_query[:, t * 128 : t * 128 + 128]
    for head in heads:
        out = jnp.where(sub, jnp.concatenate(head["grads"], 1) * HD**-0.5, head["att"])
        head["out"][...] = out.T


def call(body, outs, *args, scalar=True, scratch=(), flops=0):
    vmem = pl.BlockSpec(memory_space=pltpu.VMEM)
    specs = [vmem] * len(args)
    if scalar:
        specs[0] = pl.BlockSpec(memory_space=pltpu.SMEM)
    moved = sum(a.size * a.dtype.itemsize for a in args)
    return pl.pallas_call(
        body,
        out_shape=[jax.ShapeDtypeStruct(s, d) for s, d in outs],
        in_specs=specs,
        out_specs=[vmem] * len(outs),
        scratch_shapes=list(scratch),
        compiler_params=pltpu.CompilerParams(vmem_limit_bytes=48 * 1024 * 1024),
        cost_estimate=pl.CostEstimate(flops=flops, bytes_accessed=moved, transcendentals=0),
    )(*args)


CLASSES = (0, 16, 32, 64, 128, 256)


def interleave(own, partner):
    parts = []
    for a, b in zip(CLASSES, CLASSES[1:]):
        parts += [own[a:b], partner[a:b]]
    return jnp.concatenate(parts, 0)


def separate(rows):
    own, partner = [], []
    for a, b in zip(CLASSES, CLASSES[1:]):
        own.append(rows[2 * a : a + b])
        partner.append(rows[a + b : 2 * b])
    return jnp.concatenate(own, 0), jnp.concatenate(partner, 0)


def add_rows(arrays, blocks, extra):
    extra, start = extra.astype(F32), 0
    for n, at, size in blocks:
        piece = arrays[n][at : at + size] + extra[start : start + size]
        arrays[n] = lax.dynamic_update_slice_in_dim(arrays[n], piece, at, 0)
        start += size


def per_device(query, keys, values, grad_out):
    device = lax.axis_index("seq")
    place = jnp.stack([device & 1, ((device >> 1) ^ (device >> 2) ^ (device >> 3)) & 1]).astype(jnp.int32)
    chip_rows = gather_pair(jnp.stack([query, keys, values, grad_out]), CORE)
    send, own = call(sort_rows, [((256, 384), BF16), ((256, 512), BF16)], place, chip_rows)
    other = swap_with(send, Y_ONE)
    qg_a = interleave(own[:, :128], other[:, :128])
    qg_b = own[:, 256:384]
    kv0 = interleave(
        jnp.concatenate([own[:, 128:256], own[:, 384:]], 1), other[:, 128:]
    )
    b1 = [(0, 0, 256)]
    b2 = [(0, 0, 128), (1, 0, 128)]
    ring = [(0, 0), (1, 0), (2, 0), (2, 128)]
    b4 = [(n, at, 32) for n, at in ring]
    b3 = [(n, at, 64) for n, at in ring] + [(4, 0, 128)]
    steps = ((1, b1, Y_THREE), (2, b2, Y_SIX), (4, b4, Z_TWO), (3, b3, Z_ONE))
    kv = {0: kv0}
    for part, blocks, flip in steps:
        rows = jnp.concatenate([kv[n][at : at + size] for n, at, size in blocks], 0)
        kv[part] = swap_with(rows, flip)
    out_a, out_b, *grads = call(
        attend,
        [((512, 128), F32), ((256, 128), F32), ((512, 256), F32)]
        + [((n, 256), F32) for n in (256, 256, 384, 128)],
        qg_a, qg_b, *(kv[n] for n in range(5)),
        scalar=False,
        scratch=[
            pltpu.VMEM((1536, 512), F32), pltpu.VMEM((1536, 256), F32),
            pltpu.VMEM((1536, 512), F32), pltpu.VMEM((1536, 256), F32),
            pltpu.VMEM((128, 1536), BF16), pltpu.VMEM((128, 1536), BF16),
        ],
        flops=int(6e8),
    )
    for part, blocks, flip in reversed(steps):
        add_rows(grads, blocks, swap_with(grads[part].astype(BF16), flip))
    own_a, other_a = separate(out_a)
    own_kv, other_kv = separate(grads[0])
    send = jnp.concatenate([other_a, other_kv], 1).astype(BF16)
    own = jnp.concatenate([own_a, own_kv[:, :128], out_b, own_kv[:, 128:]], 1)
    send, keep = call(unsort_rows, [((128, 768), BF16)] * 2, place, own, swap_with(send, Y_ONE))
    return tuple(
        call(join_heads, [((128, 384), BF16)] * 4, place, keep, gather_pair(send, CORE))
    )


def solution(mesh):
    spec = P("seq", None)
    return jax.shard_map(
        per_device, mesh=mesh, in_specs=(spec,) * 4, out_specs=(spec,) * 4, check_vma=False
    )
```

```python
import jax
import jax.numpy as jnp
from jax import lax
from jax.experimental import pallas as pl
from jax.experimental.pallas import tpu as pltpu
from jax.sharding import PartitionSpec as P

HD = 64
NEG = -1e30
F32 = jnp.float32
BF16 = jnp.bfloat16

CORE, Y_ONE, Y_THREE, Y_SEVEN, Z_ONE, Z_TWO = 1, 2, 6, 14, 16, 32


def gather_pair(block, flip):
    count = lax.axis_size("seq")
    pairs = [[i, i ^ flip] for i in range(count) if i < i ^ flip]
    return lax.all_gather(block, "seq", axis_index_groups=pairs, axis=0, tiled=False)


def swap_with(block, flip):
    both = gather_pair(block, flip)
    high = 1 << (flip.bit_length() - 1)
    first = (lax.axis_index("seq") & high) == 0
    return jnp.where(first, both[1], both[0])


def dot(a, b):
    return jnp.dot(a, b, preferred_element_type=F32)


def left_half(shape):
    return lax.broadcasted_iota(jnp.int32, shape, len(shape) - 1) < HD


def pair_up(first, second, odd):
    low = left_half(first.shape)
    if odd:
        return jnp.where(low, pltpu.roll(first, HD, 1), second)
    return jnp.where(low, first, pltpu.roll(second, HD, 1))


def source_rows(shape, axis):
    i = lax.broadcasted_iota(jnp.int32, shape, axis)
    row = jnp.where(i < 64, 4 + 8 * (i - 32), jnp.where(i < 128, 2 + 4 * (i - 64), 1 + 2 * (i - 128)))
    return jnp.where(i < 16, 16 * i, jnp.where(i < 32, 8 + 16 * (i - 16), row))


def sort_rows(where_ref, x_ref, send_ref, own_ref):
    core, odd = where_ref[0], where_ref[1]

    def tile(array, h):
        cols = slice((h // 2) * 128, (h // 2) * 128 + 128)
        return jnp.concatenate([x_ref[0, array, :, cols], x_ref[1, array, :, cols]], 0).astype(F32)

    def head(h):
        q, k, v, g = (tile(array, h) for array in range(4))
        return jnp.concatenate([pair_up(q, g, h % 2), pair_up(k, v, h % 2)], 1)

    lane = lax.broadcasted_iota(jnp.int32, (256, 128), 1)
    source = source_rows((256, 128), 0)
    slots = []
    for s in range(3):
        rows = jnp.where(core == 0, head(s), head(s + 3)).astype(BF16)
        row = (source + (3 * core + s)) & 255
        order = jnp.concatenate([lane == row, lane + 128 == row], 1).astype(BF16)
        slots.append(dot(order, rows))
    send_ref[:, :256] = jnp.where(odd == 0, slots[2], slots[0]).astype(BF16)
    send_ref[:, 256:] = slots[1][:, 128:].astype(BF16)
    own_ref[:, :256] = jnp.where(odd == 0, slots[0], slots[2]).astype(BF16)
    own_ref[:, 256:] = slots[1].astype(BF16)


def unsort_rows(where_ref, own_ref, recv_ref, send_ref, keep_ref):
    core, odd = where_ref[0], where_ref[1]
    first = jnp.where(odd == 0, own_ref[:, :256], recv_ref[:, :256].astype(F32)).astype(BF16)
    third = jnp.where(odd == 0, recv_ref[:, :256].astype(F32), own_ref[:, :256]).astype(BF16)
    middle = jnp.concatenate(
        [own_ref[:, 256:384], own_ref[:, 384:] + recv_ref[:, 256:].astype(F32)], 1
    ).astype(BF16)
    sub = lax.broadcasted_iota(jnp.int32, (256, 256), 0)
    source = source_rows((1, 256), 1)
    for s, slot in enumerate((first, middle, third)):
        order = (sub == ((source + (3 * core + s)) & 255)).astype(BF16)
        rows = dot(order, slot)
        cols = slice(s * 256, s * 256 + 256)
        keep_ref[:, cols] = jnp.where(core == 0, rows[:128], rows[128:]).astype(BF16)
        send_ref[:, cols] = jnp.where(core == 0, rows[128:], rows[:128]).astype(BF16)


def join_heads(where_ref, keep_ref, recv_ref, att_ref, dq_ref, dk_ref, dv_ref):
    core = where_ref[0]
    keep, recv = keep_ref[...].astype(F32), recv_ref[1 - core].astype(F32)
    low = jnp.where(core == 0, keep, recv)
    high = jnp.where(core == 0, recv, keep)

    def part(h, p):
        half = low if h < 3 else high
        start = (h % 3) * 256 + p * 128
        return half[:, start : start + 128]

    mask = left_half((128, 128))
    for p, (left_ref, right_ref) in enumerate(((dq_ref, att_ref), (dk_ref, dv_ref))):
        for j in range(3):
            even, odd = part(2 * j, p), part(2 * j + 1, p)
            tile = slice(j * 128, j * 128 + 128)
            left_ref[:, tile] = jnp.where(mask, even, pltpu.roll(odd, HD, 1)).astype(BF16)
            right_ref[:, tile] = jnp.where(mask, pltpu.roll(even, HD, 1), odd).astype(BF16)


PIECES = (
    (0, 0, 256, 0), (0, 256, 256, None), (1, 0, 256, 1), (1, 256, 128, 2), (2, 0, 128, 2),
    (3, 0, 256, 3), (3, 256, 128, 4), (4, 0, 128, 4),
)
STARTS = (0, 512, 896, 1024, 1408)


def rank(shape, axis, step):
    i = lax.broadcasted_iota(jnp.int32, shape, axis)
    return sum((i < (step << level)).astype(F32) for level in range(4))


def key_ranks(level):
    i = lax.broadcasted_iota(jnp.int32, (256, 128), 0) & (511 >> max(level, 1))
    return sum((i < (32 << k)).astype(F32) for k in range(4))


def attend(qga_ref, qgb_ref, kv0_ref, r1_ref, r2_ref, r3_ref, r4_ref,
           outa_ref, outb_ref, d0_ref, d1_ref, d2_ref, d3_ref, d4_ref,
           ea_ref, eb_ref, pa_ref, pb_ref, ta_ref, tb_ref):
    kv_refs = (kv0_ref, r1_ref, r2_ref, r3_ref, r4_ref)
    d_refs = (d0_ref, d1_ref, d2_ref, d3_ref, d4_ref)
    sub = lax.broadcasted_iota(jnp.int32, (128, 1), 0) < HD
    ranks = [key_ranks(level) for level in (1, 2, 3)]
    heads = []
    for which, (qg_ref, out_ref, e_ref, p_ref, t_ref) in enumerate(
        ((qga_ref, outa_ref, ea_ref, pa_ref, ta_ref), (qgb_ref, outb_ref, eb_ref, pb_ref, tb_ref))
    ):
        total = qg_ref.shape[0]
        qg = qg_ref[...].astype(F32)
        low = left_half(qg.shape)
        turned = qg.T
        g_t = jnp.where(sub, 0.0, turned)
        query_rank = rank((1, 128), 1, total // 16)
        shared = [jnp.minimum(r, query_rank) for r in ranks]
        head = dict(
            total=total, out=out_ref, e=e_ref, p=p_ref, t=t_ref, g_t=g_t, g_tb=g_t.astype(BF16),
            q_t=jnp.where(sub, turned * HD**-0.5, 0.0).astype(BF16),
            q_b=jnp.where(low, qg * HD**-0.5, 0.0).astype(BF16),
            g_b=jnp.where(low, 0.0, qg).astype(BF16),
            cols=slice(which * 128, which * 128 + 128), pieces=[],
        )
        place = 0
        for part, row, rows, level in PIECES:
            width = max(128, total >> (level or 0))
            counts = [None] * (width // 128)
            if level is not None and level < 4:
                counts[0] = shared[max(level, 1) - 1][:rows] + (1.0 - level)
            if level == 0 and total == 512:
                counts[1] = 2.0
            valid = None
            if level is not None and total >> level < 128:
                valid = query_rank >= level
            head["pieces"].append((part, row, rows, width, place, counts, valid))
            place += rows
        heads.append(head)

    for head in heads:
        head["top"] = [jnp.full((1, 128), NEG, F32) for _ in range(head["total"] // 128)]
    for n in range(len(PIECES)):
        for head in heads:
            part, row, rows, width, place, counts, valid = head["pieces"][n]
            keys = kv_refs[part][row : row + rows, head["cols"]]
            start = STARTS[part] + row
            head["t"][:, start : start + rows] = keys.T
            scores = dot(keys, head["q_t"][:, :width])
            head["p"][place : place + rows, :width] = dot(keys, head["g_tb"][:, :width])
            if valid is not None:
                scores = jnp.where(valid, scores, NEG)
            head["e"][place : place + rows, :width] = scores
            top = jnp.max(scores, axis=0, keepdims=True)
            for t in range(width // 128):
                head["top"][t] = jnp.maximum(head["top"][t], top[:, t * 128 : t * 128 + 128])

    for head in heads:
        tiles = head["total"] // 128
        head["peak"] = jnp.concatenate(head["top"], 1)
        head["sums"] = [jnp.zeros((1, 128), F32) for _ in range(tiles)]
        head["accs"] = [jnp.zeros((128, 128), F32) for _ in range(tiles)]
    for n in range(len(PIECES)):
        for head in heads:
            part, row, rows, width, place, counts, valid = head["pieces"][n]
            weights = jnp.exp(head["e"][place : place + rows, :width] - head["peak"][:, :width])
            if any(count is not None for count in counts):
                cut = [weights[:, t * 128 : t * 128 + 128] for t in range(width // 128)]
                cut = [w if c is None else w * c for w, c in zip(cut, counts)]
                weights = jnp.concatenate(cut, 1)
            head["e"][place : place + rows, :width] = weights
            start = STARTS[part] + row
            acc = dot(head["t"][:, start : start + rows], weights.astype(BF16))
            added = jnp.sum(weights, axis=0, keepdims=True)
            for t in range(width // 128):
                tile = slice(t * 128, t * 128 + 128)
                head["sums"][t] = head["sums"][t] + added[:, tile]
                head["accs"][t] = head["accs"][t] + acc[:, tile]

    for head in heads:
        head["inverse"] = 1.0 / jnp.concatenate(head["sums"], 1)
        head["att"] = (jnp.concatenate(head["accs"], 1) * head["inverse"]).astype(BF16).astype(F32)
        head["delta"] = jnp.sum(head["g_t"] * head["att"], axis=0, keepdims=True)
        head["grads"] = [jnp.zeros((128, 128), F32) for _ in range(head["total"] // 128)]
    for n in range(len(PIECES)):
        for head in heads:
            part, row, rows, width, place, counts, valid = head["pieces"][n]
            probs = head["e"][place : place + rows, :width] * head["inverse"][:, :width]
            grads = probs * (head["p"][place : place + rows, :width] - head["delta"][:, :width])
            grads = grads.astype(BF16)
            both = dot(grads, head["q_b"][:width]) + dot(probs.astype(BF16), head["g_b"][:width])
            d_refs[part][row : row + rows, head["cols"]] = both
            start = STARTS[part] + row
            d_query = dot(head["t"][:, start : start + rows], grads)
            for t in range(width // 128):
                head["grads"][t] = head["grads"][t] + d_query[:, t * 128 : t * 128 + 128]
    for head in heads:
        out = jnp.where(sub, jnp.concatenate(head["grads"], 1) * HD**-0.5, head["att"])
        head["out"][...] = out.T


def call(body, outs, *args, scalar=True, scratch=(), flops=0):
    vmem = pl.BlockSpec(memory_space=pltpu.VMEM)
    specs = [vmem] * len(args)
    if scalar:
        specs[0] = pl.BlockSpec(memory_space=pltpu.SMEM)
    moved = sum(a.size * a.dtype.itemsize for a in args)
    return pl.pallas_call(
        body,
        out_shape=[jax.ShapeDtypeStruct(s, d) for s, d in outs],
        in_specs=specs,
        out_specs=[vmem] * len(outs),
        scratch_shapes=list(scratch),
        compiler_params=pltpu.CompilerParams(vmem_limit_bytes=48 * 1024 * 1024),
        cost_estimate=pl.CostEstimate(flops=flops, bytes_accessed=moved, transcendentals=0),
    )(*args)


CLASSES = (0, 16, 32, 64, 128, 256)


def interleave(own, partner):
    parts = []
    for a, b in zip(CLASSES, CLASSES[1:]):
        parts += [own[a:b], partner[a:b]]
    return jnp.concatenate(parts, 0)


def separate(rows):
    own, partner = [], []
    for a, b in zip(CLASSES, CLASSES[1:]):
        own.append(rows[2 * a : a + b])
        partner.append(rows[a + b : 2 * b])
    return jnp.concatenate(own, 0), jnp.concatenate(partner, 0)


def add_rows(arrays, blocks, extra):
    extra, start = extra.astype(F32), 0
    for n, at, size in blocks:
        piece = arrays[n][at : at + size] + extra[start : start + size]
        arrays[n] = lax.dynamic_update_slice_in_dim(arrays[n], piece, at, 0)
        start += size


def per_device(query, keys, values, grad_out):
    device = lax.axis_index("seq")
    place = jnp.stack([device & 1, ((device >> 1) ^ (device >> 2)) & 1]).astype(jnp.int32)
    chip_rows = gather_pair(jnp.stack([query, keys, values, grad_out]), CORE)
    send, own = call(sort_rows, [((256, 384), BF16), ((256, 512), BF16)], place, chip_rows)
    other = swap_with(send, Y_ONE)
    qg_a = interleave(own[:, :128], other[:, :128])
    qg_b = own[:, 256:384]
    kv0 = interleave(
        jnp.concatenate([own[:, 128:256], own[:, 384:]], 1), other[:, 128:]
    )
    ring = [(0, 0), (1, 0), (1, 256), (2, 0)]
    steps = (
        (2, [(0, 0, 128)], Y_SEVEN),
        (1, [(0, 0, 256), (2, 0, 128)], Y_THREE),
        (4, [(n, at, 32) for n, at in ring], Z_TWO),
        (3, [(n, at, 64) for n, at in ring] + [(4, 0, 128)], Z_ONE),
    )
    kv = {0: kv0}
    for part, blocks, flip in steps:
        rows = jnp.concatenate([kv[n][at : at + size] for n, at, size in blocks], 0)
        kv[part] = swap_with(rows, flip)
    out_a, out_b, *grads = call(
        attend,
        [((512, 128), F32), ((256, 128), F32), ((512, 256), F32)]
        + [((n, 256), F32) for n in (384, 128, 384, 128)],
        qg_a, qg_b, *(kv[n] for n in range(5)),
        scalar=False,
        scratch=[
            pltpu.VMEM((1536, 512), F32), pltpu.VMEM((1536, 256), F32),
            pltpu.VMEM((1536, 512), F32), pltpu.VMEM((1536, 256), F32),
            pltpu.VMEM((128, 1536), BF16), pltpu.VMEM((128, 1536), BF16),
        ],
        flops=int(6e8),
    )
    for part, blocks, flip in reversed(steps):
        add_rows(grads, blocks, swap_with(grads[part].astype(BF16), flip))
    own_a, other_a = separate(out_a)
    own_kv, other_kv = separate(grads[0])
    send = jnp.concatenate([other_a, other_kv], 1).astype(BF16)
    own = jnp.concatenate([own_a, own_kv[:, :128], out_b, own_kv[:, 128:]], 1)
    send, keep = call(unsort_rows, [((128, 768), BF16)] * 2, place, own, swap_with(send, Y_ONE))
    return tuple(
        call(join_heads, [((128, 384), BF16)] * 4, place, keep, gather_pair(send, CORE))
    )


def solution(mesh):
    spec = P("seq", None)
    return jax.shard_map(
        per_device, mesh=mesh, in_specs=(spec,) * 4, out_specs=(spec,) * 4, check_vma=False
    )
```

```python
import jax
import jax.numpy as jnp
from jax import lax
from jax.experimental import pallas as pl
from jax.experimental.pallas import tpu as pltpu
from jax.sharding import PartitionSpec as P

HD = 64
NEG = -1e30
F32 = jnp.float32
BF16 = jnp.bfloat16

CORE, Y_ONE, Y_THREE, Y_SEVEN, Z_ONE, Z_TWO = 1, 2, 6, 14, 16, 32


def gather_pair(block, flip):
    count = lax.axis_size("seq")
    pairs = [[i, i ^ flip] for i in range(count) if i < i ^ flip]
    return lax.all_gather(block, "seq", axis_index_groups=pairs, axis=0, tiled=False)


def swap_with(block, flip):
    both = gather_pair(block, flip)
    high = 1 << (flip.bit_length() - 1)
    first = (lax.axis_index("seq") & high) == 0
    return jnp.where(first, both[1], both[0])


def dot(a, b):
    return jnp.dot(a, b, preferred_element_type=F32)


def left_half(shape):
    return lax.broadcasted_iota(jnp.int32, shape, len(shape) - 1) < HD


def pair_up(first, second, odd):
    low = left_half(first.shape)
    if odd:
        return jnp.where(low, pltpu.roll(first, HD, 1), second)
    return jnp.where(low, first, pltpu.roll(second, HD, 1))


def source_rows(shape, axis):
    i = lax.broadcasted_iota(jnp.int32, shape, axis)
    row = jnp.where(i < 64, 4 + 8 * (i - 32), jnp.where(i < 128, 2 + 4 * (i - 64), 1 + 2 * (i - 128)))
    return jnp.where(i < 16, 16 * i, jnp.where(i < 32, 8 + 16 * (i - 16), row))


def own_place():
    device = lax.axis_index("seq")
    return device & 1, ((device >> 1) ^ (device >> 2)) & 1


def sort_rows(x_ref, send_ref, own_ref):
    core, odd = own_place()

    def tile(array, h):
        cols = slice((h // 2) * 128, (h // 2) * 128 + 128)
        return jnp.concatenate([x_ref[0, array, :, cols], x_ref[1, array, :, cols]], 0).astype(F32)

    def head(h):
        q, k, v, g = (tile(array, h) for array in range(4))
        return jnp.concatenate([pair_up(q, g, h % 2), pair_up(k, v, h % 2)], 1)

    lane = lax.broadcasted_iota(jnp.int32, (256, 128), 1)
    source = source_rows((256, 128), 0)
    slots = []
    for s in range(3):
        rows = jnp.where(core == 0, head(s), head(s + 3)).astype(BF16)
        row = (source + (3 * core + s)) & 255
        order = jnp.concatenate([lane == row, lane + 128 == row], 1).astype(BF16)
        slots.append(dot(order, rows))
    send_ref[:, :256] = jnp.where(odd == 0, slots[2], slots[0]).astype(BF16)
    send_ref[:, 256:] = slots[1][:, 128:].astype(BF16)
    own_ref[:, :256] = jnp.where(odd == 0, slots[0], slots[2]).astype(BF16)
    own_ref[:, 256:] = slots[1].astype(BF16)


def unsort_rows(own_ref, recv_ref, send_ref, keep_ref):
    core, odd = own_place()
    first = jnp.where(odd == 0, own_ref[:, :256], recv_ref[:, :256].astype(F32)).astype(BF16)
    third = jnp.where(odd == 0, recv_ref[:, :256].astype(F32), own_ref[:, :256]).astype(BF16)
    middle = jnp.concatenate(
        [own_ref[:, 256:384], own_ref[:, 384:] + recv_ref[:, 256:].astype(F32)], 1
    ).astype(BF16)
    sub = lax.broadcasted_iota(jnp.int32, (256, 256), 0)
    source = source_rows((1, 256), 1)
    for s, slot in enumerate((first, middle, third)):
        order = (sub == ((source + (3 * core + s)) & 255)).astype(BF16)
        rows = dot(order, slot)
        cols = slice(s * 256, s * 256 + 256)
        keep_ref[:, cols] = jnp.where(core == 0, rows[:128], rows[128:]).astype(BF16)
        send_ref[:, cols] = jnp.where(core == 0, rows[128:], rows[:128]).astype(BF16)


def join_heads(keep_ref, recv_ref, att_ref, dq_ref, dk_ref, dv_ref):
    core, _ = own_place()
    keep, recv = keep_ref[...].astype(F32), recv_ref[1 - core].astype(F32)
    low = jnp.where(core == 0, keep, recv)
    high = jnp.where(core == 0, recv, keep)

    def part(h, p):
        half = low if h < 3 else high
        start = (h % 3) * 256 + p * 128
        return half[:, start : start + 128]

    mask = left_half((128, 128))
    for p, (left_ref, right_ref) in enumerate(((dq_ref, att_ref), (dk_ref, dv_ref))):
        for j in range(3):
            even, odd = part(2 * j, p), part(2 * j + 1, p)
            tile = slice(j * 128, j * 128 + 128)
            left_ref[:, tile] = jnp.where(mask, even, pltpu.roll(odd, HD, 1)).astype(BF16)
            right_ref[:, tile] = jnp.where(mask, pltpu.roll(even, HD, 1), odd).astype(BF16)


PIECES = (
    (0, 0, 256, 0), (0, 256, 256, None), (1, 0, 256, 1), (1, 256, 128, 2), (2, 0, 128, 2),
    (3, 0, 256, 3), (3, 256, 128, 4), (4, 0, 128, 4),
)
STARTS = (0, 512, 896, 1024, 1408)


def rank(shape, axis, step):
    i = lax.broadcasted_iota(jnp.int32, shape, axis)
    return sum((i < (step << level)).astype(F32) for level in range(4))


def key_ranks(level):
    i = lax.broadcasted_iota(jnp.int32, (256, 128), 0) & (511 >> max(level, 1))
    return sum((i < (32 << k)).astype(F32) for k in range(4))


def attend(qga_ref, qgb_ref, kv0_ref, r1_ref, r2_ref, r3_ref, r4_ref,
           outa_ref, outb_ref, d0_ref, d1_ref, d2_ref, d3_ref, d4_ref,
           ea_ref, eb_ref, pa_ref, pb_ref, ta_ref, tb_ref):
    kv_refs = (kv0_ref, r1_ref, r2_ref, r3_ref, r4_ref)
    d_refs = (d0_ref, d1_ref, d2_ref, d3_ref, d4_ref)
    sub = lax.broadcasted_iota(jnp.int32, (128, 1), 0) < HD
    ranks = [key_ranks(level) for level in (1, 2, 3)]
    heads = []
    for which, (qg_ref, out_ref, e_ref, p_ref, t_ref) in enumerate(
        ((qga_ref, outa_ref, ea_ref, pa_ref, ta_ref), (qgb_ref, outb_ref, eb_ref, pb_ref, tb_ref))
    ):
        total = qg_ref.shape[0]
        qg = qg_ref[...].astype(F32)
        low = left_half(qg.shape)
        turned = qg.T
        g_t = jnp.where(sub, 0.0, turned)
        query_rank = rank((1, 128), 1, total // 16)
        shared = [jnp.minimum(r, query_rank) for r in ranks]
        head = dict(
            total=total, out=out_ref, e=e_ref, p=p_ref, t=t_ref, g_t=g_t, g_tb=g_t.astype(BF16),
            q_t=jnp.where(sub, turned * HD**-0.5, 0.0).astype(BF16),
            q_b=jnp.where(low, qg * HD**-0.5, 0.0).astype(BF16),
            g_b=jnp.where(low, 0.0, qg).astype(BF16),
            cols=slice(which * 128, which * 128 + 128), pieces=[],
        )
        place = 0
        for part, row, rows, level in PIECES:
            width = max(128, total >> (level or 0))
            counts = [None] * (width // 128)
            if level is not None and level < 4:
                counts[0] = shared[max(level, 1) - 1][:rows] + (1.0 - level)
            if level == 0 and total == 512:
                counts[1] = 2.0
            valid = None
            if level is not None and total >> level < 128:
                valid = query_rank >= level
            head["pieces"].append((part, row, rows, width, place, counts, valid))
            place += rows
        heads.append(head)

    def score(head):
        head["top"] = [jnp.full((1, 128), NEG, F32) for _ in range(head["total"] // 128)]
        for part, row, rows, width, place, counts, valid in head["pieces"]:
            keys = kv_refs[part][row : row + rows, head["cols"]]
            start = STARTS[part] + row
            head["t"][:, start : start + rows] = keys.T
            scores = dot(keys, head["q_t"][:, :width])
            head["p"][place : place + rows, :width] = dot(keys, head["g_tb"][:, :width])
            if valid is not None:
                scores = jnp.where(valid, scores, NEG)
            head["e"][place : place + rows, :width] = scores
            top = jnp.max(scores, axis=0, keepdims=True)
            for t in range(width // 128):
                head["top"][t] = jnp.maximum(head["top"][t], top[:, t * 128 : t * 128 + 128])

    def weigh(head):
        tiles = head["total"] // 128
        peak = jnp.concatenate(head["top"], 1)
        sums = [jnp.zeros((1, 128), F32) for _ in range(tiles)]
        accs = [jnp.zeros((HD, 128), F32) for _ in range(tiles)]
        for part, row, rows, width, place, counts, valid in head["pieces"]:
            weights = jnp.exp(head["e"][place : place + rows, :width] - peak[:, :width])
            if any(count is not None for count in counts):
                cut = [weights[:, t * 128 : t * 128 + 128] for t in range(width // 128)]
                cut = [w if c is None else w * c for w, c in zip(cut, counts)]
                weights = jnp.concatenate(cut, 1)
            head["e"][place : place + rows, :width] = weights
            start = STARTS[part] + row
            acc = dot(head["t"][HD:, start : start + rows], weights.astype(BF16))
            added = jnp.sum(weights, axis=0, keepdims=True)
            for t in range(width // 128):
                tile = slice(t * 128, t * 128 + 128)
                sums[t] = sums[t] + added[:, tile]
                accs[t] = accs[t] + acc[:, tile]
        head["inverse"] = 1.0 / jnp.concatenate(sums, 1)
        head["att"] = (jnp.concatenate(accs, 1) * head["inverse"]).astype(BF16).astype(F32)
        head["delta"] = jnp.sum(head["g_t"][HD:] * head["att"], axis=0, keepdims=True)

    def differentiate(head):
        grads_q = [jnp.zeros((HD, 128), F32) for _ in range(head["total"] // 128)]
        for part, row, rows, width, place, counts, valid in head["pieces"]:
            probs = head["e"][place : place + rows, :width] * head["inverse"][:, :width]
            grads = probs * (head["p"][place : place + rows, :width] - head["delta"][:, :width])
            grads = grads.astype(BF16)
            both = dot(grads, head["q_b"][:width]) + dot(probs.astype(BF16), head["g_b"][:width])
            d_refs[part][row : row + rows, head["cols"]] = both
            start = STARTS[part] + row
            d_query = dot(head["t"][:HD, start : start + rows], grads)
            for t in range(width // 128):
                grads_q[t] = grads_q[t] + d_query[:, t * 128 : t * 128 + 128]
        out = jnp.concatenate([jnp.concatenate(grads_q, 1) * HD**-0.5, head["att"]], 0)
        head["out"][...] = out.T

    longer, shorter = heads
    score(shorter)
    score(longer)
    weigh(shorter)
    weigh(longer)
    differentiate(shorter)
    differentiate(longer)


def call(body, outs, *args, scratch=(), flops=0):
    vmem = pl.BlockSpec(memory_space=pltpu.VMEM)
    specs = [vmem] * len(args)
    moved = sum(a.size * a.dtype.itemsize for a in args)
    return pl.pallas_call(
        body,
        out_shape=[jax.ShapeDtypeStruct(s, d) for s, d in outs],
        in_specs=specs,
        out_specs=[vmem] * len(outs),
        scratch_shapes=list(scratch),
        compiler_params=pltpu.CompilerParams(vmem_limit_bytes=48 * 1024 * 1024),
        cost_estimate=pl.CostEstimate(flops=flops, bytes_accessed=moved, transcendentals=0),
    )(*args)


CLASSES = (0, 16, 32, 64, 128, 256)


def interleave(own, partner):
    parts = []
    for a, b in zip(CLASSES, CLASSES[1:]):
        parts += [own[a:b], partner[a:b]]
    return jnp.concatenate(parts, 0)


def separate(rows):
    own, partner = [], []
    for a, b in zip(CLASSES, CLASSES[1:]):
        own.append(rows[2 * a : a + b])
        partner.append(rows[a + b : 2 * b])
    return jnp.concatenate(own, 0), jnp.concatenate(partner, 0)


def add_rows(arrays, blocks, extra):
    extra, start = extra.astype(F32), 0
    for n, at, size in blocks:
        piece = arrays[n][at : at + size] + extra[start : start + size]
        arrays[n] = lax.dynamic_update_slice_in_dim(arrays[n], piece, at, 0)
        start += size


def per_device(query, keys, values, grad_out):
    chip_rows = gather_pair(jnp.stack([query, keys, values, grad_out]), CORE)
    send, own = call(sort_rows, [((256, 384), BF16), ((256, 512), BF16)], chip_rows)
    other = swap_with(send, Y_ONE)
    qg_a = interleave(own[:, :128], other[:, :128])
    qg_b = own[:, 256:384]
    kv0 = interleave(
        jnp.concatenate([own[:, 128:256], own[:, 384:]], 1), other[:, 128:]
    )
    ring = [(0, 0), (1, 0), (1, 256), (2, 0)]
    steps = (
        (2, [(0, 0, 128)], Y_SEVEN),
        (1, [(0, 0, 256), (2, 0, 128)], Y_THREE),
        (4, [(n, at, 32) for n, at in ring], Z_TWO),
        (3, [(n, at, 64) for n, at in ring] + [(4, 0, 128)], Z_ONE),
    )
    kv = {0: kv0}
    for part, blocks, flip in steps:
        rows = jnp.concatenate([kv[n][at : at + size] for n, at, size in blocks], 0)
        kv[part] = swap_with(rows, flip)
    out_a, out_b, *grads = call(
        attend,
        [((512, 128), F32), ((256, 128), F32), ((512, 256), F32)]
        + [((n, 256), F32) for n in (384, 128, 384, 128)],
        qg_a, qg_b, *(kv[n] for n in range(5)),
        scratch=[
            pltpu.VMEM((1536, 512), F32), pltpu.VMEM((1536, 256), F32),
            pltpu.VMEM((1536, 512), F32), pltpu.VMEM((1536, 256), F32),
            pltpu.VMEM((128, 1536), BF16), pltpu.VMEM((128, 1536), BF16),
        ],
        flops=int(6e8),
    )
    for part, blocks, flip in reversed(steps):
        add_rows(grads, blocks, swap_with(grads[part].astype(BF16), flip))
    own_a, other_a = separate(out_a)
    own_kv, other_kv = separate(grads[0])
    send = jnp.concatenate([other_a, other_kv], 1).astype(BF16)
    own = jnp.concatenate([own_a, own_kv[:, :128], out_b, own_kv[:, 128:]], 1)
    send, keep = call(unsort_rows, [((128, 768), BF16)] * 2, own, swap_with(send, Y_ONE))
    return tuple(
        call(join_heads, [((128, 384), BF16)] * 4, keep, gather_pair(send, CORE))
    )


def solution(mesh):
    spec = P("seq", None)
    return jax.shard_map(
        per_device, mesh=mesh, in_specs=(spec,) * 4, out_specs=(spec,) * 4, check_vma=False
    )
```

```python
import jax
import jax.numpy as jnp
from jax import lax
from jax.experimental import pallas as pl
from jax.experimental.pallas import tpu as pltpu
from jax.sharding import PartitionSpec as P

HD = 64
NEG = -1e30
F32 = jnp.float32
BF16 = jnp.bfloat16

CORE, Y_ONE, Y_THREE, Y_SEVEN, Z_ONE, Z_TWO = 1, 2, 6, 14, 16, 32


def gather_pair(block, flip):
    count = lax.axis_size("seq")
    pairs = [[i, i ^ flip] for i in range(count) if i < i ^ flip]
    return lax.all_gather(block, "seq", axis_index_groups=pairs, axis=0, tiled=False)


def swap_with(block, flip):
    both = gather_pair(block, flip)
    high = 1 << (flip.bit_length() - 1)
    first = (lax.axis_index("seq") & high) == 0
    return jnp.where(first, both[1], both[0])


def dot(a, b):
    return jnp.dot(a, b, preferred_element_type=F32)


def left_half(shape):
    return lax.broadcasted_iota(jnp.int32, shape, len(shape) - 1) < HD


def pair_up(first, second, odd):
    low = left_half(first.shape)
    if odd:
        return jnp.where(low, pltpu.roll(first, HD, 1), second)
    return jnp.where(low, first, pltpu.roll(second, HD, 1))


def source_rows(shape, axis):
    i = lax.broadcasted_iota(jnp.int32, shape, axis)
    row = jnp.where(i < 64, 4 + 8 * (i - 32), jnp.where(i < 128, 2 + 4 * (i - 64), 1 + 2 * (i - 128)))
    return jnp.where(i < 16, 16 * i, jnp.where(i < 32, 8 + 16 * (i - 16), row))


def own_place():
    device = lax.axis_index("seq")
    return device & 1, ((device >> 1) ^ (device >> 2)) & 1


def sort_rows(x_ref, send_ref, own_ref):
    core, odd = own_place()

    def tile(array, h):
        cols = slice((h // 2) * 128, (h // 2) * 128 + 128)
        return jnp.concatenate([x_ref[0, array, :, cols], x_ref[1, array, :, cols]], 0).astype(F32)

    def head(h):
        q, k, v, g = (tile(array, h) for array in range(4))
        return jnp.concatenate([pair_up(q, g, h % 2), pair_up(k, v, h % 2)], 1)

    lane = lax.broadcasted_iota(jnp.int32, (256, 128), 1)
    source = source_rows((256, 128), 0)
    slots = []
    for s in range(3):
        rows = jnp.where(core == 0, head(s), head(s + 3)).astype(BF16)
        row = (source + (3 * core + s)) & 255
        order = jnp.concatenate([lane == row, lane + 128 == row], 1).astype(BF16)
        slots.append(dot(order, rows))
    send_ref[:, :256] = jnp.where(odd == 0, slots[2], slots[0]).astype(BF16)
    send_ref[:, 256:] = slots[1][:, 128:].astype(BF16)
    own_ref[:, :256] = jnp.where(odd == 0, slots[0], slots[2]).astype(BF16)
    own_ref[:, 256:384] = slots[1][:, 128:].astype(BF16)
    own_ref[:, 384:] = slots[1][:, :128].astype(BF16)


def unsort_rows(a_ref, b_ref, d_ref, recv_ref, send_ref, keep_ref):
    core, odd = own_place()
    mine = jnp.concatenate([a_ref[...], d_ref[:, :128].astype(BF16)], 1)
    first = jnp.where(odd == 0, mine, recv_ref[:, :256])
    third = jnp.where(odd == 0, recv_ref[:, :256], mine)
    shared = d_ref[:, 128:] + recv_ref[:, 256:].astype(F32)
    middle = jnp.concatenate([b_ref[...], shared.astype(BF16)], 1)
    sub = lax.broadcasted_iota(jnp.int32, (256, 256), 0)
    source = source_rows((1, 256), 1)
    for s, slot in enumerate((first, middle, third)):
        order = (sub == ((source + (3 * core + s)) & 255)).astype(BF16)
        rows = dot(order, slot)
        cols = slice(s * 256, s * 256 + 256)
        keep_ref[:, cols] = jnp.where(core == 0, rows[:128], rows[128:]).astype(BF16)
        send_ref[:, cols] = jnp.where(core == 0, rows[128:], rows[:128]).astype(BF16)


def join_heads(keep_ref, recv_ref, att_ref, dq_ref, dk_ref, dv_ref):
    core, _ = own_place()
    keep, recv = keep_ref[...].astype(F32), recv_ref[1 - core].astype(F32)
    low = jnp.where(core == 0, keep, recv)
    high = jnp.where(core == 0, recv, keep)

    def part(h, p):
        half = low if h < 3 else high
        start = (h % 3) * 256 + p * 128
        return half[:, start : start + 128]

    mask = left_half((128, 128))
    for p, (left_ref, right_ref) in enumerate(((dq_ref, att_ref), (dk_ref, dv_ref))):
        for j in range(3):
            even, odd = part(2 * j, p), part(2 * j + 1, p)
            tile = slice(j * 128, j * 128 + 128)
            left_ref[:, tile] = jnp.where(mask, even, pltpu.roll(odd, HD, 1)).astype(BF16)
            right_ref[:, tile] = jnp.where(mask, pltpu.roll(even, HD, 1), odd).astype(BF16)


PIECES = (
    (0, 0, 256, 0), (0, 256, 256, None), (1, 0, 256, 1), (1, 256, 128, 2), (2, 0, 128, 2),
    (3, 0, 256, 3), (3, 256, 128, 4), (4, 0, 128, 4),
)
STARTS = (0, 512, 896, 1024, 1408)


def rank(shape, axis, step):
    i = lax.broadcasted_iota(jnp.int32, shape, axis)
    return sum((i < (step << level)).astype(F32) for level in range(4))


def key_ranks(level):
    i = lax.broadcasted_iota(jnp.int32, (256, 128), 0) & (127 >> max(level - 1, 0))
    return sum((i < (16 << k)).astype(F32) for k in range(4))


CLASSES = (0, 16, 32, 64, 128, 256)


def interleave(own, partner):
    parts = []
    for a, b in zip(CLASSES, CLASSES[1:]):
        parts += [own[a:b], partner[a:b]]
    return jnp.concatenate(parts, 0)


def attend(own_ref, other_ref, qgb_ref, kv0_ref, r1_ref, r2_ref, r3_ref, r4_ref, kv5_ref,
           outa_ref, outo_ref, outb_ref, d0_ref, d1_ref, d2_ref, d3_ref, d4_ref, d5_ref,
           ea_ref, eb_ref, pa_ref, pb_ref, ta_ref, tb_ref):
    kv_refs = (None, r1_ref, r2_ref, r3_ref, r4_ref)
    d_refs = (None, d1_ref, d2_ref, d3_ref, d4_ref)

    def keys_of(part, row, rows, cols):
        if part:
            return kv_refs[part][row : row + rows, cols]
        half = slice(row // 2, row // 2 + 128)
        return jnp.concatenate([kv0_ref[half, cols], kv5_ref[half, cols]], 0)

    def put(part, row, rows, cols, both):
        if part:
            d_refs[part][row : row + rows, cols] = both
        else:
            half = slice(row // 2, row // 2 + 128)
            d0_ref[half, cols] = both[:128]
            d5_ref[half, cols] = both[128:]

    sub = lax.broadcasted_iota(jnp.int32, (128, 1), 0) < HD
    ranks = [key_ranks(level) for level in (1, 2, 3)]
    heads = []
    pair = interleave(own_ref[...], other_ref[...])
    for which, (qg, e_ref, p_ref, t_ref) in enumerate(
        ((pair, ea_ref, pa_ref, ta_ref), (qgb_ref[...], eb_ref, pb_ref, tb_ref))
    ):
        total = qg.shape[0]
        qg = qg.astype(F32)
        low = left_half(qg.shape)
        turned = qg.T
        g_t = jnp.where(sub, 0.0, turned)
        query_rank = rank((1, 128), 1, total // 16)
        shared = [jnp.minimum(r, query_rank) for r in ranks]
        head = dict(
            total=total, e=e_ref, p=p_ref, t=t_ref, g_t=g_t, g_tb=g_t.astype(BF16),
            q_t=jnp.where(sub, turned * HD**-0.5, 0.0).astype(BF16),
            q_b=jnp.where(low, qg * HD**-0.5, 0.0).astype(BF16),
            g_b=jnp.where(low, 0.0, qg).astype(BF16),
            cols=slice(which * 128, which * 128 + 128), pieces=[],
        )
        place = 0
        for part, row, rows, level in PIECES:
            width = max(128, total >> (level or 0))
            counts = [None] * (width // 128)
            if level is not None and level < 4:
                counts[0] = shared[max(level, 1) - 1][:rows] + (1.0 - level)
            if level == 0 and total == 512:
                counts[1] = 2.0
            valid = None
            if level is not None and total >> level < 128:
                valid = query_rank >= level
            head["pieces"].append((part, row, rows, width, place, counts, valid))
            place += rows
        heads.append(head)

    def score(head):
        head["top"] = [jnp.full((1, 128), NEG, F32) for _ in range(head["total"] // 128)]
        for part, row, rows, width, place, counts, valid in head["pieces"]:
            keys = keys_of(part, row, rows, head["cols"])
            start = STARTS[part] + row
            head["t"][:, start : start + rows] = keys.T
            scores = dot(keys, head["q_t"][:, :width])
            head["p"][place : place + rows, :width] = dot(keys, head["g_tb"][:, :width])
            if valid is not None:
                scores = jnp.where(valid, scores, NEG)
            head["e"][place : place + rows, :width] = scores
            top = jnp.max(scores, axis=0, keepdims=True)
            for t in range(width // 128):
                head["top"][t] = jnp.maximum(head["top"][t], top[:, t * 128 : t * 128 + 128])

    def weigh(head):
        tiles = head["total"] // 128
        peak = jnp.concatenate(head["top"], 1)
        sums = [jnp.zeros((1, 128), F32) for _ in range(tiles)]
        accs = [jnp.zeros((HD, 128), F32) for _ in range(tiles)]
        for part, row, rows, width, place, counts, valid in head["pieces"]:
            weights = jnp.exp(head["e"][place : place + rows, :width] - peak[:, :width])
            if any(count is not None for count in counts):
                cut = [weights[:, t * 128 : t * 128 + 128] for t in range(width // 128)]
                cut = [w if c is None else w * c for w, c in zip(cut, counts)]
                weights = jnp.concatenate(cut, 1)
            head["e"][place : place + rows, :width] = weights
            start = STARTS[part] + row
            acc = dot(head["t"][HD:, start : start + rows], weights.astype(BF16))
            added = jnp.sum(weights, axis=0, keepdims=True)
            for t in range(width // 128):
                tile = slice(t * 128, t * 128 + 128)
                sums[t] = sums[t] + added[:, tile]
                accs[t] = accs[t] + acc[:, tile]
        head["inverse"] = 1.0 / jnp.concatenate(sums, 1)
        head["att"] = (jnp.concatenate(accs, 1) * head["inverse"]).astype(BF16).astype(F32)
        head["delta"] = jnp.sum(head["g_t"][HD:] * head["att"], axis=0, keepdims=True)

    def differentiate(head):
        grads_q = [jnp.zeros((HD, 128), F32) for _ in range(head["total"] // 128)]
        for part, row, rows, width, place, counts, valid in head["pieces"]:
            probs = head["e"][place : place + rows, :width] * head["inverse"][:, :width]
            grads = probs * (head["p"][place : place + rows, :width] - head["delta"][:, :width])
            grads = grads.astype(BF16)
            both = dot(grads, head["q_b"][:width]) + dot(probs.astype(BF16), head["g_b"][:width])
            put(part, row, rows, head["cols"], both)
            start = STARTS[part] + row
            d_query = dot(head["t"][:HD, start : start + rows], grads)
            for t in range(width // 128):
                grads_q[t] = grads_q[t] + d_query[:, t * 128 : t * 128 + 128]
        out = jnp.concatenate([jnp.concatenate(grads_q, 1) * HD**-0.5, head["att"]], 0)
        return out.T.astype(BF16)

    longer, shorter = heads
    score(shorter)
    score(longer)
    weigh(shorter)
    weigh(longer)
    outb_ref[...] = differentiate(shorter)
    out = differentiate(longer)
    for a, b in zip(CLASSES, CLASSES[1:]):
        outa_ref[a:b] = out[2 * a : a + b]
        outo_ref[a:b] = out[a + b : 2 * b]


def call(body, outs, *args, scratch=(), flops=0):
    vmem = pl.BlockSpec(memory_space=pltpu.VMEM)
    specs = [vmem] * len(args)
    moved = sum(a.size * a.dtype.itemsize for a in args)
    return pl.pallas_call(
        body,
        out_shape=[jax.ShapeDtypeStruct(s, d) for s, d in outs],
        in_specs=specs,
        out_specs=[vmem] * len(outs),
        scratch_shapes=list(scratch),
        compiler_params=pltpu.CompilerParams(vmem_limit_bytes=48 * 1024 * 1024),
        cost_estimate=pl.CostEstimate(flops=flops, bytes_accessed=moved, transcendentals=0),
    )(*args)


def add_rows(arrays, blocks, extra):
    extra, start = extra.astype(F32), 0
    for n, at, size in blocks:
        piece = arrays[n][at : at + size] + extra[start : start + size]
        arrays[n] = lax.dynamic_update_slice_in_dim(arrays[n], piece, at, 0)
        start += size


def per_device(query, keys, values, grad_out):
    chip_rows = gather_pair(jnp.stack([query, keys, values, grad_out]), CORE)
    send, own = call(sort_rows, [((256, 384), BF16), ((256, 512), BF16)], chip_rows)
    other = swap_with(send, Y_ONE)
    kv = {0: own[:, 128:384], 5: other[:, 128:]}
    ring = [(0, 0), (5, 0), (1, 0), (1, 128), (1, 256), (1, 320), (2, 0), (2, 64)]
    steps = (
        (2, [(0, 0, 64), (5, 0, 64)], Y_SEVEN),
        (1, [(0, 0, 128), (5, 0, 128), (2, 0, 128)], Y_THREE),
        (4, [(n, at, 16) for n, at in ring], Z_TWO),
        (3, [(n, at, 32) for n, at in ring] + [(4, 0, 128)], Z_ONE),
    )
    for part, blocks, flip in steps:
        rows = jnp.concatenate([kv[n][at : at + size] for n, at, size in blocks], 0)
        kv[part] = swap_with(rows, flip)
    *outs, d0, d1, d2, d3, d4, d5 = call(
        attend,
        [((256, 128), BF16)] * 3 + [((n, 256), F32) for n in (256, 384, 128, 384, 128, 256)],
        own[:, :128], other[:, :128], own[:, 384:], *(kv[n] for n in range(6)),
        scratch=[
            pltpu.VMEM((1536, 512), F32), pltpu.VMEM((1536, 256), F32),
            pltpu.VMEM((1536, 512), F32), pltpu.VMEM((1536, 256), F32),
            pltpu.VMEM((128, 1536), BF16), pltpu.VMEM((128, 1536), BF16),
        ],
        flops=int(6e8),
    )
    grads = [d0, d1, d2, d3, d4, d5]
    for part, blocks, flip in reversed(steps):
        add_rows(grads, blocks, swap_with(grads[part].astype(BF16), flip))
    send = jnp.concatenate([outs[1], grads[5].astype(BF16)], 1)
    send, keep = call(unsort_rows, [((128, 768), BF16)] * 2, outs[0], outs[2], grads[0], swap_with(send, Y_ONE))
    return tuple(
        call(join_heads, [((128, 384), BF16)] * 4, keep, gather_pair(send, CORE))
    )


def solution(mesh):
    spec = P("seq", None)
    return jax.shard_map(
        per_device, mesh=mesh, in_specs=(spec,) * 4, out_specs=(spec,) * 4, check_vma=False
    )
```

```python
import jax
import jax.numpy as jnp
from jax import lax
from jax.experimental import pallas as pl
from jax.experimental.pallas import tpu as pltpu
from jax.sharding import PartitionSpec as P

HD = 64
NEG = -1e30
F32 = jnp.float32
BF16 = jnp.bfloat16

CORE, Y_ONE, Y_THREE, Y_SEVEN, Z_ONE, Z_TWO = 1, 2, 6, 14, 16, 32


def gather_pair(block, flip):
    count = lax.axis_size("seq")
    pairs = [[i, i ^ flip] for i in range(count) if i < i ^ flip]
    return lax.all_gather(block, "seq", axis_index_groups=pairs, axis=0, tiled=False)


def swap_with(block, flip):
    both = gather_pair(block, flip)
    high = 1 << (flip.bit_length() - 1)
    first = (lax.axis_index("seq") & high) == 0
    return jnp.where(first, both[1], both[0])


def dot(a, b):
    return jnp.dot(a, b, preferred_element_type=F32)


def left_half(shape):
    return lax.broadcasted_iota(jnp.int32, shape, len(shape) - 1) < HD


def pair_up(first, second, odd):
    low = left_half(first.shape)
    if odd:
        return jnp.where(low, pltpu.roll(first, HD, 1), second)
    return jnp.where(low, first, pltpu.roll(second, HD, 1))


def source_rows(shape, axis):
    i = lax.broadcasted_iota(jnp.int32, shape, axis)
    row = jnp.where(i < 64, 4 + 8 * (i - 32), jnp.where(i < 128, 2 + 4 * (i - 64), 1 + 2 * (i - 128)))
    return jnp.where(i < 16, 16 * i, jnp.where(i < 32, 8 + 16 * (i - 16), row))


def own_place():
    device = lax.axis_index("seq")
    return device & 1, ((device >> 1) ^ (device >> 2)) & 1


def sort_rows(x_ref, send_ref, own_ref):
    core, odd = own_place()

    def tile(array, h):
        cols = slice((h // 2) * 128, (h // 2) * 128 + 128)
        return jnp.concatenate([x_ref[0, array, :, cols], x_ref[1, array, :, cols]], 0).astype(F32)

    def head(h):
        q, k, v, g = (tile(array, h) for array in range(4))
        return jnp.concatenate([pair_up(q, g, h % 2), pair_up(k, v, h % 2)], 1)

    lane = lax.broadcasted_iota(jnp.int32, (256, 128), 1)
    source = source_rows((256, 128), 0)
    slots = []
    for s in range(3):
        rows = jnp.where(core == 0, head(s), head(s + 3)).astype(BF16)
        row = (source + (3 * core + s)) & 255
        order = jnp.concatenate([lane == row, lane + 128 == row], 1).astype(BF16)
        slots.append(dot(order, rows))
    send_ref[:, :256] = jnp.where(odd == 0, slots[2], slots[0]).astype(BF16)
    send_ref[:, 256:] = slots[1][:, 128:].astype(BF16)
    own_ref[:, :256] = jnp.where(odd == 0, slots[0], slots[2]).astype(BF16)
    own_ref[:, 256:384] = slots[1][:, 128:].astype(BF16)
    own_ref[:, 384:] = slots[1][:, :128].astype(BF16)


def unsort_rows(a_ref, b_ref, d_ref, recv_ref, send_ref, keep_ref):
    core, odd = own_place()
    mine = jnp.concatenate([a_ref[...], d_ref[:, :128].astype(BF16)], 1)
    first = jnp.where(odd == 0, mine, recv_ref[:, :256])
    third = jnp.where(odd == 0, recv_ref[:, :256], mine)
    shared = d_ref[:, 128:] + recv_ref[:, 256:].astype(F32)
    middle = jnp.concatenate([b_ref[...], shared.astype(BF16)], 1)
    sub = lax.broadcasted_iota(jnp.int32, (256, 256), 0)
    source = source_rows((1, 256), 1)
    for s, slot in enumerate((first, middle, third)):
        order = (sub == ((source + (3 * core + s)) & 255)).astype(BF16)
        rows = dot(order, slot)
        cols = slice(s * 256, s * 256 + 256)
        keep_ref[:, cols] = jnp.where(core == 0, rows[:128], rows[128:]).astype(BF16)
        send_ref[:, cols] = jnp.where(core == 0, rows[128:], rows[:128]).astype(BF16)


def join_heads(keep_ref, recv_ref, att_ref, dq_ref, dk_ref, dv_ref):
    core, _ = own_place()
    keep, recv = keep_ref[...].astype(F32), recv_ref[1 - core].astype(F32)
    low = jnp.where(core == 0, keep, recv)
    high = jnp.where(core == 0, recv, keep)

    def part(h, p):
        half = low if h < 3 else high
        start = (h % 3) * 256 + p * 128
        return half[:, start : start + 128]

    mask = left_half((128, 128))
    for p, (left_ref, right_ref) in enumerate(((dq_ref, att_ref), (dk_ref, dv_ref))):
        for j in range(3):
            even, odd = part(2 * j, p), part(2 * j + 1, p)
            tile = slice(j * 128, j * 128 + 128)
            left_ref[:, tile] = jnp.where(mask, even, pltpu.roll(odd, HD, 1)).astype(BF16)
            right_ref[:, tile] = jnp.where(mask, pltpu.roll(even, HD, 1), odd).astype(BF16)


PIECES = (
    (0, 0, 256, 0), (0, 256, 256, None), (1, 0, 256, 1), (1, 256, 128, 2), (2, 0, 128, 2),
    (3, 0, 256, 3), (3, 256, 128, 4), (4, 0, 128, 4),
)
STARTS = (0, 512, 896, 1024, 1408)


def rank(shape, axis, step):
    i = lax.broadcasted_iota(jnp.int32, shape, axis)
    return sum((i < (step << level)).astype(F32) for level in range(4))


def key_ranks(level):
    i = lax.broadcasted_iota(jnp.int32, (256, 128), 0) & (127 >> max(level - 1, 0))
    return sum((i < (16 << k)).astype(F32) for k in range(4))


CLASSES = (0, 16, 32, 64, 128, 256)


def interleave(own, partner):
    parts = []
    for a, b in zip(CLASSES, CLASSES[1:]):
        parts += [own[a:b], partner[a:b]]
    return jnp.concatenate(parts, 0)


def attend(own_ref, other_ref, qgb_ref, kv0_ref, r1_ref, r2_ref, r3_ref, r4_ref, kv5_ref,
           outa_ref, outo_ref, outb_ref, d0_ref, d1_ref, d2_ref, d3_ref, d4_ref, d5_ref,
           ea_ref, eb_ref, pa_ref, pb_ref, ta_ref, tb_ref):
    kv_refs = (None, r1_ref, r2_ref, r3_ref, r4_ref)
    d_refs = (None, d1_ref, d2_ref, d3_ref, d4_ref)

    def keys_of(part, row, rows, cols):
        if part:
            return kv_refs[part][row : row + rows, cols]
        half = slice(row // 2, row // 2 + 128)
        return jnp.concatenate([kv0_ref[half, cols], kv5_ref[half, cols]], 0)

    def put(part, row, rows, cols, both):
        if part:
            d_refs[part][row : row + rows, cols] = both.astype(d_refs[part].dtype)
        else:
            half = slice(row // 2, row // 2 + 128)
            d0_ref[half, cols] = both[:128]
            d5_ref[half, cols] = both[128:]

    sub = lax.broadcasted_iota(jnp.int32, (128, 1), 0) < HD
    ranks = [key_ranks(level) for level in (1, 2, 3)]
    heads = []
    pair = interleave(own_ref[...], other_ref[...])
    for which, (qg, e_ref, p_ref, t_ref) in enumerate(
        ((pair, ea_ref, pa_ref, ta_ref), (qgb_ref[...], eb_ref, pb_ref, tb_ref))
    ):
        total = qg.shape[0]
        qg = qg.astype(F32)
        low = left_half(qg.shape)
        turned = qg.T
        g_t = jnp.where(sub, 0.0, turned)
        query_rank = rank((1, 128), 1, total // 16)
        shared = [jnp.minimum(r, query_rank) for r in ranks]
        head = dict(
            total=total, e=e_ref, p=p_ref, t=t_ref, g_t=g_t, g_tb=g_t.astype(BF16),
            q_t=jnp.where(sub, turned * HD**-0.5, 0.0).astype(BF16),
            q_b=jnp.where(low, qg * HD**-0.5, 0.0).astype(BF16),
            g_b=jnp.where(low, 0.0, qg).astype(BF16),
            cols=slice(which * 128, which * 128 + 128), pieces=[],
        )
        place = 0
        for part, row, rows, level in PIECES:
            width = max(128, total >> (level or 0))
            counts = [None] * (width // 128)
            if level is not None and level < 4:
                counts[0] = shared[max(level, 1) - 1][:rows] + (1.0 - level)
            if level == 0 and total == 512:
                counts[1] = 2.0
            valid = None
            if level is not None and total >> level < 128:
                valid = query_rank >= level
            head["pieces"].append((part, row, rows, width, place, counts, valid))
            place += rows
        heads.append(head)

    def score(head):
        head["top"] = [jnp.full((1, 128), NEG, F32) for _ in range(head["total"] // 128)]
        for part, row, rows, width, place, counts, valid in head["pieces"]:
            keys = keys_of(part, row, rows, head["cols"])
            start = STARTS[part] + row
            head["t"][:, start : start + rows] = keys.T
            scores = dot(keys, head["q_t"][:, :width])
            head["p"][place : place + rows, :width] = dot(keys, head["g_tb"][:, :width])
            if valid is not None:
                scores = jnp.where(valid, scores, NEG)
            head["e"][place : place + rows, :width] = scores
            top = jnp.max(scores, axis=0, keepdims=True)
            for t in range(width // 128):
                head["top"][t] = jnp.maximum(head["top"][t], top[:, t * 128 : t * 128 + 128])

    def weigh(head):
        tiles = head["total"] // 128
        peak = jnp.concatenate(head["top"], 1)
        sums = [jnp.zeros((1, 128), F32) for _ in range(tiles)]
        accs = [jnp.zeros((HD, 128), F32) for _ in range(tiles)]
        for part, row, rows, width, place, counts, valid in head["pieces"]:
            weights = jnp.exp(head["e"][place : place + rows, :width] - peak[:, :width])
            if any(count is not None for count in counts):
                cut = [weights[:, t * 128 : t * 128 + 128] for t in range(width // 128)]
                cut = [w if c is None else w * c for w, c in zip(cut, counts)]
                weights = jnp.concatenate(cut, 1)
            head["e"][place : place + rows, :width] = weights
            start = STARTS[part] + row
            acc = dot(head["t"][HD:, start : start + rows], weights.astype(BF16))
            added = jnp.sum(weights, axis=0, keepdims=True)
            for t in range(width // 128):
                tile = slice(t * 128, t * 128 + 128)
                sums[t] = sums[t] + added[:, tile]
                accs[t] = accs[t] + acc[:, tile]
        head["inverse"] = 1.0 / jnp.concatenate(sums, 1)
        head["att"] = (jnp.concatenate(accs, 1) * head["inverse"]).astype(BF16).astype(F32)
        head["delta"] = jnp.sum(head["g_t"][HD:] * head["att"], axis=0, keepdims=True)

    def differentiate(head):
        grads_q = [jnp.zeros((HD, 128), F32) for _ in range(head["total"] // 128)]
        for part, row, rows, width, place, counts, valid in head["pieces"]:
            probs = head["e"][place : place + rows, :width] * head["inverse"][:, :width]
            grads = probs * (head["p"][place : place + rows, :width] - head["delta"][:, :width])
            grads = grads.astype(BF16)
            both = dot(grads, head["q_b"][:width]) + dot(probs.astype(BF16), head["g_b"][:width])
            put(part, row, rows, head["cols"], both)
            start = STARTS[part] + row
            d_query = dot(head["t"][:HD, start : start + rows], grads)
            for t in range(width // 128):
                grads_q[t] = grads_q[t] + d_query[:, t * 128 : t * 128 + 128]
        out = jnp.concatenate([jnp.concatenate(grads_q, 1) * HD**-0.5, head["att"]], 0)
        return out.T.astype(BF16)

    longer, shorter = heads
    score(shorter)
    score(longer)
    weigh(shorter)
    weigh(longer)
    outb_ref[...] = differentiate(shorter)
    out = differentiate(longer)
    for a, b in zip(CLASSES, CLASSES[1:]):
        outa_ref[a:b] = out[2 * a : a + b]
        outo_ref[a:b] = out[a + b : 2 * b]


def call(body, outs, *args, scratch=(), flops=0):
    vmem = pl.BlockSpec(memory_space=pltpu.VMEM)
    specs = [vmem] * len(args)
    moved = sum(a.size * a.dtype.itemsize for a in args)
    return pl.pallas_call(
        body,
        out_shape=[jax.ShapeDtypeStruct(s, d) for s, d in outs],
        in_specs=specs,
        out_specs=[vmem] * len(outs),
        scratch_shapes=list(scratch),
        compiler_params=pltpu.CompilerParams(vmem_limit_bytes=48 * 1024 * 1024),
        cost_estimate=pl.CostEstimate(flops=flops, bytes_accessed=moved, transcendentals=0),
    )(*args)


def add_rows(arrays, blocks, extra):
    extra, start = extra.astype(F32), 0
    for n, at, size in blocks:
        piece = arrays[n][at : at + size] + extra[start : start + size]
        arrays[n] = lax.dynamic_update_slice_in_dim(arrays[n], piece, at, 0)
        start += size


def per_device(query, keys, values, grad_out):
    chip_rows = gather_pair(jnp.stack([query, keys, values, grad_out]), CORE)
    send, own = call(sort_rows, [((256, 384), BF16), ((256, 512), BF16)], chip_rows)
    other = swap_with(send, Y_ONE)
    kv = {0: own[:, 128:384], 5: other[:, 128:]}
    ring = [(0, 0), (5, 0), (1, 0), (1, 128), (1, 256), (1, 320), (2, 0), (2, 64)]
    steps = (
        (2, [(0, 0, 64), (5, 0, 64)], Y_SEVEN),
        (1, [(0, 0, 128), (5, 0, 128), (2, 0, 128)], Y_THREE),
        (4, [(n, at, 16) for n, at in ring], Z_TWO),
        (3, [(n, at, 32) for n, at in ring] + [(4, 0, 128)], Z_ONE),
    )
    for part, blocks, flip in steps:
        rows = jnp.concatenate([kv[n][at : at + size] for n, at, size in blocks], 0)
        kv[part] = swap_with(rows, flip)
    *outs, d0, d1, d2, d3, d4, d5 = call(
        attend,
        [((256, 128), BF16)] * 3
        + [((n, 256), BF16 if part == 3 else F32) for part, n in enumerate((256, 384, 128, 384, 128, 256))],
        own[:, :128], other[:, :128], own[:, 384:], *(kv[n] for n in range(6)),
        scratch=[
            pltpu.VMEM((1536, 512), F32), pltpu.VMEM((1536, 256), F32),
            pltpu.VMEM((1536, 512), F32), pltpu.VMEM((1536, 256), F32),
            pltpu.VMEM((128, 1536), BF16), pltpu.VMEM((128, 1536), BF16),
        ],
        flops=int(6e8),
    )
    grads = [d0, d1, d2, d3, d4, d5]
    for part, blocks, flip in reversed(steps):
        add_rows(grads, blocks, swap_with(grads[part].astype(BF16), flip))
    send = jnp.concatenate([outs[1], grads[5].astype(BF16)], 1)
    send, keep = call(unsort_rows, [((128, 768), BF16)] * 2, outs[0], outs[2], grads[0], swap_with(send, Y_ONE))
    return tuple(
        call(join_heads, [((128, 384), BF16)] * 4, keep, gather_pair(send, CORE))
    )


def solution(mesh):
    spec = P("seq", None)
    return jax.shard_map(
        per_device, mesh=mesh, in_specs=(spec,) * 4, out_specs=(spec,) * 4, check_vma=False
    )
```
